32 devices in a mesh: own: 16 (over z, x, core), blk: 2 (over y).
Axes of the slice: x: 2, y: 2, z: 4, core: 2. Of those that a mesh axis runs over, the one named last changes fastest.
Arguments:
- amplitudes: bfloat16 [16, 3072, 3072], P('own', 'blk'), may hold values from -6 to 6
- amp_mask: int32 [16, 24, 24], P('own', 'blk'), may hold values 0 or 1
- bare_ints: bfloat16 [16, 3072, 3072], P('own', 'blk'), may hold values from -6 to 6
- int_tiles: bfloat16 [2, 16, 10, 128, 128], P('blk', 'own'), may hold values from -0.375 to 0.375
- tile_ids: int32 [2, 16, 10], P('blk', 'own'), may hold values from -1 to 287, as said below
- eps_virt: float32 [3072], replicated, may hold values from 0.5 to 3
- eps_pair: float32 [16], P('own'), may hold values from -2 to -0.5
Outputs:
- new_amps: bfloat16 [16, 3072, 3072], P('own', 'blk')
The draws below stay inside these ranges and needn't reach their ends.
Inputs may be any that keep to these rules, and one draw needn't show every extreme that they name: `tile_ids`: each entry is -1 or id = a * 24 + c for a live tile at row a of the block's 12 tile rows and column c; each position appears at most once in a block; each block of index g has exactly 32 live tiles, among them always the last position; no device holds more than 10, and in every block one device holds exactly 10.
All inputs are finite; a program needn't handle non-finite values. No bound on the sum of `amp_mask` on one device may be relied on, other than what follows from the above.
Results may differ from the reference program's by a relative error of at most 0.001.
Values may be sent and summed in bfloat16 or wider, within the bound.
No kernel may reach another device: no remote copies, remote signals or barrier semaphores. Data moves between devices by JAX's collectives and lax.ppermute only.
A program may use at most 128 MiB of HBM per device.

```python
import jax
import jax.numpy as jnp
from jax import lax

TILE = 128
NT = 24
OWN_CAP = 10
NV = 3072
LIVE = 32
NPAIR = 16
N_OWN = 16
N_BLK = 2


def draw_tile_ids(key, part):
    row_tiles = NT // N_BLK
    positions_all = row_tiles * NT
    others = (N_OWN - 1) * OWN_CAP

    def one_block(block_key):
        key_pos, key_heavy, key_slots, key_mix = jax.random.split(block_key, 4)
        rest_pos = jax.random.permutation(key_pos, positions_all - 1)[:LIVE - 1].astype(jnp.int32)
        last_pos = jnp.full((1,), positions_all - 1, jnp.int32)
        picked = jax.random.permutation(key_mix, jnp.concatenate([last_pos, rest_pos], axis=0)).astype(jnp.int32)
        heavy = jax.random.randint(key_heavy, (), 0, N_OWN).astype(jnp.int32)
        chosen = jax.random.permutation(key_slots, others)[:LIVE - OWN_CAP]
        rest = jnp.full((others,), -1, jnp.int32).at[chosen].set(picked[OWN_CAP:])
        rows = jnp.concatenate([picked[:OWN_CAP][None, :], rest.reshape(N_OWN - 1, OWN_CAP)], axis=0)
        order = (jnp.arange(N_OWN, dtype=jnp.int32) - heavy) % N_OWN
        return rows[order]
    return jax.vmap(one_block)(jax.random.split(key, N_BLK))


def set_ends(values, stream_key, least, largest):
    longest = values.shape.index(max(values.shape))
    spots = []
    for shift in (0, 1):
        where = [jax.random.randint(jax.random.fold_in(stream_key, axis), (), 0, length) for axis, length in enumerate(values.shape)]
        where[longest] = (where[longest] + shift) % values.shape[longest]
        spots.append(tuple(where))
    return values.at[spots[0]].set(least).at[spots[1]].set(largest)


def block_levels(key, shape, cuts, least, top_value):
    loudness = 1.0
    for axis_at, shards_of in cuts:
        steps = jax.random.uniform(jax.random.fold_in(jax.random.fold_in(key, 6), axis_at), (shards_of,), jnp.float32, least / len(cuts), top_value / len(cuts))
        loudness = loudness * jnp.repeat(jnp.exp(steps), shape[axis_at] // shards_of).reshape((-1,) + (1,) * (len(shape) - 1 - axis_at))
    return loudness


def scatter_about(stream_key, shape, scale, bound, shards=(), held_as=jnp.bfloat16):
    array = scale * jax.random.normal(stream_key, shape, jnp.float32)
    if shards:
        array = array * block_levels(stream_key, shape, shards, -0.22, 0.18)
    return jnp.clip(array, -bound, bound).astype(held_as)


def setup_inputs(seed: int = 0) -> dict:
    arg_keys = jax.random.split(jax.random.key(seed), 8)
    amplitudes = scatter_about(arg_keys[0], (NPAIR, NV, NV), 1.0, 6.0, ((0, 16), (1, 2)))
    amp_mask = set_ends((jax.random.randint(arg_keys[1], (NPAIR, NT, NT), 0, 4) < 3).astype(jnp.int32), jax.random.fold_in(arg_keys[1], 1), 0, 1)
    bare_ints = scatter_about(arg_keys[2], (NPAIR, NV, NV), 1.0, 6.0, ((0, 16), (1, 2)))
    int_tiles = scatter_about(arg_keys[3], (N_BLK, N_OWN, OWN_CAP, TILE, TILE), ((LIVE * N_BLK // NT) * TILE) ** -0.5, 0.375, ((0, 2), (1, 16)))
    tile_ids = draw_tile_ids(jax.random.fold_in(arg_keys[7], 71), 0)
    eps_virt = jnp.clip(jax.random.uniform(arg_keys[5], (NV,), jnp.float32, 0.5, 3.0), 0.5, 3.0)
    eps_pair = jnp.clip(-2.0 + 1.5 * jax.random.uniform(arg_keys[6], (NPAIR,), jnp.float32) ** block_levels(arg_keys[6], (NPAIR,), ((0, 16),), -0.2, 0.2), -2.0, -0.5)
    return dict(amplitudes=amplitudes, amp_mask=amp_mask, bare_ints=bare_ints, int_tiles=int_tiles, tile_ids=tile_ids, eps_virt=eps_virt, eps_pair=eps_pair)


def reference(amplitudes, amp_mask, bare_ints, int_tiles, tile_ids, eps_virt, eps_pair):
    row_tiles = NT // N_BLK
    flat_ids = tile_ids.reshape(N_BLK, -1)
    block = jnp.arange(N_BLK, dtype=jnp.int32)[:, None]
    position = jnp.where(flat_ids >= 0, block * (row_tiles * NT) + flat_ids, NT * NT).astype(jnp.int32).reshape(-1)
    tiles = int_tiles.reshape(-1, TILE, TILE).astype(jnp.float32)
    grid = jnp.zeros((NT * NT, TILE, TILE), jnp.float32).at[position].add(tiles, mode="drop")
    wmat = grid.reshape(NT, NT, TILE, TILE).transpose(0, 2, 1, 3).reshape(NT * TILE, NT * TILE)

    def one_pair(items):
        amps, mask, bare, pair_energy = items
        mask_el = jnp.repeat(jnp.repeat(mask, TILE, axis=0), TILE, axis=1).astype(jnp.float32)
        screened = amps.astype(jnp.float32) * mask_el
        cycle = jnp.dot(wmat, screened, precision=lax.Precision.HIGHEST)
        denom = eps_virt[:, None] + eps_virt[None, :] - pair_energy
        return (((bare.astype(jnp.float32) + cycle) / denom) * mask_el).astype(jnp.bfloat16)

    return lax.map(one_pair, (amplitudes, amp_mask, bare_ints, eps_pair))
```

```python
import functools

import jax
import jax.numpy as jnp
from jax import lax
from jax.experimental import pallas as pl
from jax.experimental.pallas import tpu as pltpu
from jax.sharding import PartitionSpec as P

TILE = 128
NT = 24
STEP = 2
EARLY = 2
CHUNKS = (40, 40, 32)
GRAIN = 16
ROWS = 512
VMEM = 48 * 1024 * 1024


def passed_along(value, axis, steps):
    count = lax.axis_size(axis)
    pairs = [(source, (source + steps) % count) for source in range(count)]
    return lax.ppermute(value, axis, pairs)


def by24(index):
    return (index * 2731) >> 16


def plan_and_pack(row_tiles, cap, early, chunks, grain, where, info, amps, plan_out, *rest):
    n_chunks = len(chunks)
    extra = rest[0]
    bufs = rest[1 : 1 + n_chunks]
    plan, plan_sem, pack_sem = rest[1 + n_chunks :]
    width = info.shape[2]
    live = row_tiles * NT
    own, blk = where[0], where[1]
    row = lax.broadcasted_iota(jnp.int32, (width, width), 0)
    lane = lax.broadcasted_iota(jnp.int32, (width, width), 1)
    row_hi, lane_hi = by24(row), by24(lane)
    row_lo, lane_lo = row - row_hi * NT, lane - lane_hi * NT
    same_lo = (row_lo == lane_lo).astype(jnp.float32)
    row_key, lane_key = row_lo * row_tiles + row_hi, lane_lo * row_tiles + lane_hi
    ahead = ((row_lo >= early) & (row_key < lane_key) & (row < live)).astype(jnp.bfloat16)
    lanes = lax.broadcasted_iota(jnp.int32, (16, width), 1)
    lanes_lo = lanes - by24(lanes) * NT
    places = lax.broadcasted_iota(jnp.int32, (8, width), 1)
    places_hi = by24(places)
    which = lax.broadcasted_iota(jnp.int32, (8, width), 0)
    digits = jnp.where(which == 0, places_hi, jnp.where(which == 1, places - places_hi * NT, 0))
    digits = digits.astype(jnp.bfloat16)
    owners = info.shape[1]
    mine = (lax.broadcasted_iota(jnp.int32, (owners, 1), 0) == own).astype(jnp.float32)
    lanes = lax.broadcasted_iota(jnp.int32, (owners, width), 1)
    lanes_lo = lanes - by24(lanes) * NT
    most = jnp.int32(0)
    found = []
    for g in range(2):
        h = 1 - g
        seen = jnp.zeros((owners, width), jnp.float32)
        for slot in range(cap):
            seen = seen + (info[g, :, live + slot : live + slot + 1] == lanes).astype(jnp.float32)
        seen = jnp.sum(seen, axis=0, keepdims=True)
        left = jnp.where(row_hi == lane_hi, seen, 0.0).astype(jnp.bfloat16)
        right = (row_lo == h * row_tiles + lane_hi).astype(jnp.bfloat16)
        meets = jnp.dot(left, right, preferred_element_type=jnp.float32) * same_lo
        kept_rows = jnp.where(lanes < live, info[g], 0).astype(jnp.bfloat16)
        hits = jnp.dot(kept_rows, meets.astype(jnp.bfloat16), preferred_element_type=jnp.float32)
        kept_columns = jnp.where(lanes < live, info[h], 0)
        need = jnp.where((hits > 0.5) & (kept_columns > 0), 1.0, 0.0)
        late = jnp.where(lanes_lo >= early, need, 0.0)
        count = jnp.sum(late, axis=1, keepdims=True)
        most = jnp.maximum(most, jnp.max(count).astype(jnp.int32))
        my_late = jnp.sum(late * mine, axis=0, keepdims=True)
        my_count = jnp.sum(my_late, axis=1, keepdims=True)
        before = jnp.dot(my_late.astype(jnp.bfloat16), ahead, preferred_element_type=jnp.float32)
        before_column = lax.dot_general(
            ahead, jnp.broadcast_to(my_late, (8, width)).astype(jnp.bfloat16),
            (((0,), (1,)), ((), ())), preferred_element_type=jnp.float32,
        )[:, :1]
        late_column = jnp.sum(jnp.where(row == lane, my_late, 0.0), axis=1, keepdims=True)
        onehot = jnp.where(before_column == lane.astype(jnp.float32), late_column, 0.0)
        listed = jnp.dot(digits, onehot.astype(jnp.bfloat16), preferred_element_type=jnp.float32)
        found.append((listed[0:1], listed[1:2], before, jnp.broadcast_to(my_count, (1, width))))
    mask = [
        jnp.sum(jnp.where(lanes < live, info[g], 0).astype(jnp.float32) * mine, axis=0, keepdims=True)
        for g in range(2)
    ]
    first = blk == 0
    received = [jnp.where(first, a, b) for a, b in zip(found[0], found[1])]
    sent = [jnp.where(first, b, a) for a, b in zip(found[0], found[1])]
    lines = [
        sent[0], sent[1], sent[3], received[0], received[1], received[2], received[3],
        jnp.where(first, mask[0], mask[1]), jnp.where(first, mask[1], mask[0]),
    ]
    for index, line in enumerate(lines):
        plan_out[index : index + 1, :] = line.astype(jnp.int32)
    plan_out[9:10, :] = jnp.broadcast_to(most, (1, width))
    copy = pltpu.make_async_copy(plan_out, plan, plan_sem)
    copy.start()
    copy.wait()
    total = plan[2, 0]
    shift = rest_of(plan[9, 0], chunks, grain)

    def tile_copy(slot, target):
        place = pl.multiple_of(plan[0, slot] * TILE, TILE), pl.multiple_of(plan[1, slot] * TILE, TILE)
        return pltpu.make_async_copy(
            amps.at[0, pl.ds(place[0], TILE), pl.ds(place[1], TILE)], target, pack_sem
        )

    def pack(buf, start, stop):
        def one(slot, carry):
            tile_copy(slot, buf.at[slot - start]).start()
            return carry

        lax.fori_loop(start, jnp.maximum(stop, start), one, 0)

    pack(extra, jnp.int32(0), jnp.minimum(shift, total))
    start = shift
    for buf, size in zip(bufs, chunks):
        pack(buf, start, jnp.minimum(start + size, total))
        start = start + size

    def done(slot, carry):
        tile_copy(0, extra.at[0]).wait()
        return carry

    lax.fori_loop(0, total, done, 0)


def rest_of(most, chunks, grain):
    over = jnp.maximum(most - sum(chunks), 0)
    return (over + grain - 1) // grain * grain


def place_kernel(part, whole, sem):
    copy = pltpu.make_async_copy(part, whole.at[pl.ds(0, part.shape[0])], sem)
    copy.start()
    copy.wait()


def placed(part, size):
    return pl.pallas_call(
        place_kernel,
        out_shape=jax.ShapeDtypeStruct((size,) + part.shape[1:], part.dtype),
        in_specs=[pl.BlockSpec(memory_space=pl.ANY)],
        out_specs=pl.BlockSpec(memory_space=pl.ANY),
        scratch_shapes=[pltpu.SemaphoreType.DMA],
        name="placed",
    )(part)


def cycle_kernel(
    row_tiles, cap, early, chunks, grain, stage, where, plan, labels, energy, eps_row, eps_col,
    tiles, amps, bare, early_buf, prev_buf, this_buf, out_in, out, w, xl, xr, held, made, sems, w_sem,
):
    del out_in
    blk = where[1]
    live = row_tiles * NT
    steps = NT // STEP
    cols = STEP * TILE
    shift = rest_of(plan[9, 0], chunks, grain)
    total = plan[6, 0]

    def slot_at(column):
        return jnp.where(column >= NT, total, plan[5, jnp.minimum(column, NT - 1)])

    def complete(limit):
        def one(step, count):
            return count + (slot_at((step + 1) * STEP) <= limit).astype(jnp.int32)

        return lax.fori_loop(0, steps, one, jnp.int32(0))

    ends = [shift + sum(chunks[:index]) for index in range(len(chunks) + 1)]
    begin = jnp.int32(0) if stage == 0 else complete(ends[stage])
    end = jnp.int32(steps) if stage == len(chunks) - 1 else complete(ends[stage + 1])
    split = ends[stage]
    prev_start = 0 if stage == 0 else ends[stage - 1]

    def dense_copies(step, slot):
        at = pl.ds(pl.multiple_of(step * cols, cols), cols)
        return (
            pltpu.make_async_copy(amps.at[0, :, at], xl.at[slot], sems.at[0, slot]),
            pltpu.make_async_copy(bare.at[0, :, at], held.at[slot], sems.at[1, slot]),
        )

    def out_copy(step, slot):
        at = pl.ds(pl.multiple_of(step * cols, cols), cols)
        return pltpu.make_async_copy(made.at[slot], out.at[0, :, at], sems.at[3, slot])

    def tile_copy(source, place, column, slot):
        rows = pl.ds(pl.multiple_of(place * TILE, TILE), TILE)
        at = pl.ds(pl.multiple_of(column * TILE, TILE), TILE)
        return pltpu.make_async_copy(source, xr.at[slot, rows, at], sems.at[2, slot])

    def early_copy(step, slot):
        at = pl.ds(pl.multiple_of(step * cols, cols), cols)
        return pltpu.make_async_copy(early_buf.at[0, :, at], xr.at[slot], sems.at[2, slot])

    def issue(step, slot):
        for copy in dense_copies(step, slot):
            copy.start()
        is_early = step * STEP < early

        def tiles_in():
            xr[slot] = jnp.zeros(xr.shape[1:], xr.dtype)
            low, high = slot_at(step * STEP), slot_at((step + 1) * STEP)

            def from_buf(buf, base):
                def one(index, carry):
                    tile_copy(buf.at[index - base], plan[3, index], plan[4, index] - step * STEP, slot).start()
                    return carry

                return one

            middle = jnp.clip(split, low, high)
            lax.fori_loop(low, middle, from_buf(prev_buf, prev_start), 0)
            lax.fori_loop(middle, high, from_buf(this_buf, split), 0)

        if stage == 0 and early:
            pl.when(is_early)(lambda: early_copy(step, slot).start())
            pl.when(jnp.logical_not(is_early))(tiles_in)
        else:
            tiles_in()

    def masked(ref, line, step, slot):
        def one(place, carry):
            rows = pl.ds(pl.multiple_of(place * TILE, TILE), TILE)
            for column in range(STEP):
                kept = plan[line, place * NT + step * STEP + column]

                @pl.when(kept == 0)
                def _():
                    ref[slot, rows, column * TILE : (column + 1) * TILE] = jnp.zeros((TILE, TILE), ref.dtype)

            return carry

        lax.fori_loop(0, row_tiles, one, 0)

    def arrive(step, slot):
        for copy in dense_copies(step, slot):
            copy.wait()
        masked(xl, 7, step, slot)

        def tiles_wait():
            def one(index, carry):
                tile_copy(this_buf.at[0], 0, 0, slot).wait()
                return carry

            lax.fori_loop(slot_at(step * STEP), slot_at((step + 1) * STEP), one, 0)

        def early_wait():
            early_copy(step, slot).wait()
            masked(xr, 8, step, slot)

        if stage == 0 and early:
            is_early = step * STEP < early
            pl.when(is_early)(early_wait)
            pl.when(jnp.logical_not(is_early))(tiles_wait)
        else:
            tiles_wait()

    def product(step, slot):
        at = pl.ds(pl.multiple_of(step * cols, cols), cols)
        half = row_tiles * TILE

        def one(block, carry):
            rows = pl.ds(pl.multiple_of(block * ROWS, ROWS), ROWS)
            acc = jnp.dot(w[rows, :half], xl[slot], preferred_element_type=jnp.float32)
            acc = acc + jnp.dot(w[rows, half:], xr[slot], preferred_element_type=jnp.float32)
            denom = eps_row[rows, :] + eps_col[:, at] - energy[0]
            value = (held[slot, rows, :].astype(jnp.float32) + acc) / denom
            for part in range(ROWS // TILE):
                for column in range(STEP):
                    kept = plan[7, (block * (ROWS // TILE) + part) * NT + step * STEP + column]
                    piece = value[part * TILE : (part + 1) * TILE, column * TILE : (column + 1) * TILE]
                    place = pl.ds(pl.multiple_of(block * ROWS + part * TILE, TILE), TILE)
                    made[slot, place, column * TILE : (column + 1) * TILE] = (
                        piece * kept.astype(jnp.float32)
                    ).astype(made.dtype)
            return carry

        lax.fori_loop(0, half // ROWS, one, 0)

    def w_copy(slot, row_at, column_at):
        rows = pl.ds(pl.multiple_of(row_at * TILE, TILE), TILE)
        at = pl.ds(pl.multiple_of(column_at * TILE, TILE), TILE)
        return pltpu.make_async_copy(tiles.at[slot], w.at[rows, at], w_sem)

    @pl.when(begin < end)
    def _():
        issue(begin, lax.rem(begin, 2))

        def clear(place, carry):
            w[pl.ds(pl.multiple_of(place * TILE, TILE), TILE), :] = jnp.zeros((TILE, w.shape[1]), w.dtype)
            return carry

        lax.fori_loop(0, row_tiles, clear, 0)
        owners = labels.shape[0]

        def of_owner(owner, count):
            for position in range(cap):
                label = labels[owner, live + position]

                @pl.when(label >= 0)
                def _():
                    place = by24(label)
                    column = label - place * NT - blk * row_tiles
                    w_copy(owner * cap + position, place, jnp.where(column < 0, column + NT, column)).start()

                count = count + (label >= 0).astype(jnp.int32)
            return count

        started = lax.fori_loop(0, owners, of_owner, jnp.int32(0))

        def landed(index, carry):
            w_copy(0, 0, 0).wait()
            return carry

        lax.fori_loop(0, started, landed, 0)

        def one(step, carry):
            slot = lax.rem(step, 2)

            @pl.when(step + 1 < end)
            def _():
                issue(step + 1, 1 - slot)

            arrive(step, slot)

            @pl.when(step >= begin + 2)
            def _():
                out_copy(step - 2, slot).wait()

            product(step, slot)
            out_copy(step, slot).start()
            return carry

        lax.fori_loop(begin, end, one, 0)

        @pl.when(end >= begin + 2)
        def _():
            out_copy(end - 2, lax.rem(end, 2)).wait()

        out_copy(end - 1, lax.rem(end - 1, 2)).wait()


def screened_exchange(amplitudes, amp_mask, bare_ints, int_tiles, tile_ids, eps_virt, eps_pair):
    pairs, panel_rows, width = amplitudes.shape
    row_tiles = panel_rows // TILE
    cap = tile_ids.shape[2]
    owners = lax.axis_size("own")
    own, blk = lax.axis_index("own"), lax.axis_index("blk")
    where = jnp.stack([own, blk]).astype(jnp.int32)
    early, chunks, grain = EARLY, CHUNKS, GRAIN
    most_extra = row_tiles * (NT - early) - sum(chunks)
    branches = -(-most_extra // grain)
    any_space = pl.BlockSpec(memory_space=pl.ANY)
    smem = pl.BlockSpec(memory_space=pltpu.SMEM)
    vmem = pl.BlockSpec(memory_space=pltpu.VMEM)

    early_buf = passed_along(amplitudes[:, :, : early * TILE], "blk", 1)
    tiles = lax.all_gather(int_tiles, "own", axis=1, tiled=True).reshape(-1, TILE, TILE)

    live = row_tiles * NT
    wide = -(-(live + cap) // TILE) * TILE
    told = jnp.concatenate([amp_mask.reshape(1, -1), tile_ids.reshape(1, -1)], axis=1)
    told = jnp.pad(told, ((0, 0), (0, wide - live - cap)), constant_values=-1)
    told = jnp.broadcast_to(told, (2 * owners, wide))
    info = lax.all_to_all(told, ("blk", "own"), 0, 0, tiled=True).reshape(2, owners, wide)

    tile_type = lambda count: jax.ShapeDtypeStruct((count, TILE, TILE), amplitudes.dtype)
    plan, extra, *bufs = pl.pallas_call(
        functools.partial(plan_and_pack, row_tiles, cap, early, chunks, grain),
        out_shape=[jax.ShapeDtypeStruct((16, wide), jnp.int32), tile_type(branches * grain)]
        + [tile_type(size) for size in chunks],
        in_specs=[smem, vmem, any_space],
        out_specs=[vmem] + [any_space] * (1 + len(chunks)),
        scratch_shapes=[pltpu.SMEM((16, wide), jnp.int32), pltpu.SemaphoreType.DMA, pltpu.SemaphoreType.DMA],
        compiler_params=pltpu.CompilerParams(vmem_limit_bytes=VMEM),
        name="plan_and_pack",
    )(where, info, amplitudes)

    def branch(index):
        def send(buf):
            if index == 0:
                return buf
            return placed(passed_along(buf[: index * grain], "blk", 1), buf.shape[0])

        return send

    shift = rest_of(plan[9, 0], chunks, grain)
    got = lax.switch(shift // grain, [branch(index) for index in range(branches + 1)], extra)
    bufs = [passed_along(buf, "blk", 1) for buf in bufs]

    labels = lax.dynamic_index_in_dim(info, blk, 0, keepdims=False)
    eps_row = lax.dynamic_slice_in_dim(eps_virt, blk * panel_rows, panel_rows, 0).reshape(panel_rows, 1)
    eps_col = eps_virt.reshape(1, width)
    cols = STEP * TILE
    out = None
    for stage in range(len(chunks)):
        prev_buf = got if stage == 0 else bufs[stage - 1]
        operands = [
            where, plan, labels, eps_pair, eps_row, eps_col, tiles, amplitudes, bare_ints, early_buf,
            prev_buf, bufs[stage], bare_ints if out is None else out,
        ]
        specs = [smem, smem, smem, smem, vmem, vmem] + [any_space] * 7
        out = pl.pallas_call(
            functools.partial(cycle_kernel, row_tiles, cap, early, chunks, grain, stage),
            out_shape=jax.ShapeDtypeStruct(amplitudes.shape, amplitudes.dtype),
            in_specs=specs,
            out_specs=any_space,
            input_output_aliases={} if out is None else {12: 0},
            scratch_shapes=[
                pltpu.VMEM((panel_rows, width), jnp.bfloat16),
                pltpu.VMEM((2, panel_rows, cols), jnp.bfloat16),
                pltpu.VMEM((2, panel_rows, cols), jnp.bfloat16),
                pltpu.VMEM((2, panel_rows, cols), jnp.bfloat16),
                pltpu.VMEM((2, panel_rows, cols), jnp.bfloat16),
                pltpu.SemaphoreType.DMA((4, 2)),
                pltpu.SemaphoreType.DMA,
            ],
            compiler_params=pltpu.CompilerParams(vmem_limit_bytes=VMEM),
            cost_estimate=pl.CostEstimate(
                flops=2 * panel_rows * width * width // len(chunks),
                bytes_accessed=4 * panel_rows * width * 2 // len(chunks),
                transcendentals=0,
            ),
            name=f"cycle_{stage}",
        )(*operands)
    return out


def ring_exchange(amplitudes, amp_mask, bare_ints, int_tiles, tile_ids, eps_virt, eps_pair):
    pairs, panel_rows, width = amplitudes.shape
    row_tiles = panel_rows // TILE
    slots = row_tiles * NT
    mask_cells = jnp.broadcast_to(
        amp_mask.astype(jnp.bfloat16)[:, :, None, :, None], (pairs, row_tiles, TILE, NT, TILE)
    ).reshape(pairs, panel_rows, width)
    screened = amplitudes * mask_cells
    tiles = lax.all_gather(int_tiles, "own", axis=1, tiled=True)
    labels = lax.all_gather(tile_ids, "own", axis=1, tiled=True)
    flat_labels = labels.reshape(-1)
    flat_tiles = tiles.reshape(-1, TILE, TILE)
    onehot = (flat_labels[:, None] == jnp.arange(slots, dtype=jnp.int32)[None, :]).astype(jnp.bfloat16)
    grid = jnp.einsum("sq,sij->qij", onehot, flat_tiles, preferred_element_type=jnp.float32)
    w_rows = (
        grid.astype(jnp.bfloat16)
        .reshape(row_tiles, NT, TILE, TILE)
        .transpose(0, 2, 1, 3)
        .reshape(panel_rows, width)
    )
    position = lax.axis_index("blk")
    stops = lax.axis_size("blk")
    panel = screened
    cycle_sum = jnp.zeros((pairs, panel_rows, width), jnp.float32)
    for stop in range(stops):
        columns = lax.dynamic_slice_in_dim(w_rows, (position - stop) % stops * panel_rows, panel_rows, 1)
        cycle_sum = cycle_sum + jnp.einsum("ac,pcb->pab", columns, panel, preferred_element_type=jnp.float32)
        if stop + 1 < stops:
            panel = passed_along(panel, "blk", 1)
    rows_energy = lax.dynamic_slice_in_dim(eps_virt, position * panel_rows, panel_rows, 0)
    denom = rows_energy[None, :, None] + eps_virt[None, None, :] - eps_pair[:, None, None]
    updated = (bare_ints.astype(jnp.float32) + cycle_sum) / denom * mask_cells.astype(jnp.float32)
    return updated.astype(jnp.bfloat16)


def solution(mesh):
    local = screened_exchange if mesh.shape["blk"] == 2 else ring_exchange
    in_specs = (
        P("own", "blk", None),
        P("own", "blk", None),
        P("own", "blk", None),
        P("blk", "own", None, None, None),
        P("blk", "own", None),
        P(),
        P("own"),
    )
    out_specs = P("own", "blk", None)
    return jax.shard_map(local, mesh=mesh, in_specs=in_specs, out_specs=out_specs, check_vma=False)
```

```python
import functools

import jax
import jax.numpy as jnp
from jax import lax
from jax.experimental import pallas as pl
from jax.experimental.pallas import tpu as pltpu
from jax.sharding import PartitionSpec as P

TILE = 128
NT = 24
STEP = 2
EARLY = 2
CHUNKS = (40, 40, 32)
GRAIN = 16
ROWS = 256
GROUP = 8
VMEM = 62 * 1024 * 1024
VMEM_CYCLE = 52 * 1024 * 1024


def passed_along(value, axis, steps):
    count = lax.axis_size(axis)
    pairs = [(source, (source + steps) % count) for source in range(count)]
    return lax.ppermute(value, axis, pairs)


def by24(index):
    return (index * 2731) >> 16


def make_plan(
    row_tiles, cap, early, where, info, plan_out,
):
    width = info.shape[2]
    live = row_tiles * NT
    own, blk = where[0], where[1]
    row = lax.broadcasted_iota(jnp.int32, (width, width), 0)
    lane = lax.broadcasted_iota(jnp.int32, (width, width), 1)
    row_hi, lane_hi = by24(row), by24(lane)
    row_lo, lane_lo = row - row_hi * NT, lane - lane_hi * NT
    same_lo = (row_lo == lane_lo).astype(jnp.float32)
    row_key, lane_key = row_lo * row_tiles + row_hi, lane_lo * row_tiles + lane_hi
    ahead = ((row_lo >= early) & (row_key < lane_key) & (row < live)).astype(jnp.bfloat16)
    lanes = lax.broadcasted_iota(jnp.int32, (16, width), 1)
    lanes_lo = lanes - by24(lanes) * NT
    places = lax.broadcasted_iota(jnp.int32, (8, width), 1)
    places_hi = by24(places)
    which = lax.broadcasted_iota(jnp.int32, (8, width), 0)
    digits = jnp.where(which == 0, places_hi, jnp.where(which == 1, places - places_hi * NT, 0))
    digits = digits.astype(jnp.bfloat16)
    owners = info.shape[1]
    mine = (lax.broadcasted_iota(jnp.int32, (owners, 1), 0) == own).astype(jnp.float32)
    lanes = lax.broadcasted_iota(jnp.int32, (owners, width), 1)
    lanes_lo = lanes - by24(lanes) * NT
    most = jnp.int32(0)
    found = []
    for g in range(2):
        h = 1 - g
        seen = jnp.zeros((owners, width), jnp.float32)
        for slot in range(cap):
            seen = seen + (info[g, :, live + slot : live + slot + 1] == lanes).astype(jnp.float32)
        seen = jnp.sum(seen, axis=0, keepdims=True)
        left = jnp.where(row_hi == lane_hi, seen, 0.0).astype(jnp.bfloat16)
        right = (row_lo == h * row_tiles + lane_hi).astype(jnp.bfloat16)
        meets = jnp.dot(left, right, preferred_element_type=jnp.float32) * same_lo
        kept_rows = jnp.where(lanes < live, info[g], 0).astype(jnp.bfloat16)
        hits = jnp.dot(kept_rows, meets.astype(jnp.bfloat16), preferred_element_type=jnp.float32)
        kept_columns = jnp.where(lanes < live, info[h], 0)
        need = jnp.where((hits > 0.5) & (kept_columns > 0), 1.0, 0.0)
        late = jnp.where(lanes_lo >= early, need, 0.0)
        count = jnp.sum(late, axis=1, keepdims=True)
        most = jnp.maximum(most, jnp.max(count).astype(jnp.int32))
        my_late = jnp.sum(late * mine, axis=0, keepdims=True)
        my_count = jnp.sum(my_late, axis=1, keepdims=True)
        before = jnp.dot(my_late.astype(jnp.bfloat16), ahead, preferred_element_type=jnp.float32)
        before_column = lax.dot_general(
            ahead, jnp.broadcast_to(my_late, (8, width)).astype(jnp.bfloat16),
            (((0,), (1,)), ((), ())), preferred_element_type=jnp.float32,
        )[:, :1]
        late_column = jnp.sum(jnp.where(row == lane, my_late, 0.0), axis=1, keepdims=True)
        onehot = jnp.where(before_column == lane.astype(jnp.float32), late_column, 0.0)
        listed = jnp.dot(digits, onehot.astype(jnp.bfloat16), preferred_element_type=jnp.float32)
        found.append((listed[0:1], listed[1:2], before, jnp.broadcast_to(my_count, (1, width))))
    mask = [
        jnp.sum(jnp.where(lanes < live, info[g], 0).astype(jnp.float32) * mine, axis=0, keepdims=True)
        for g in range(2)
    ]
    first = blk == 0
    received = [jnp.where(first, a, b) for a, b in zip(found[0], found[1])]
    sent = [jnp.where(first, b, a) for a, b in zip(found[0], found[1])]
    lines = [
        sent[0], sent[1], sent[3], received[0], received[1], received[2], received[3],
        jnp.where(first, mask[0], mask[1]), jnp.where(first, mask[1], mask[0]),
    ]
    for index, line in enumerate(lines):
        plan_out[index : index + 1, :] = line.astype(jnp.int32)
    plan_out[9:10, :] = jnp.broadcast_to(most, (1, width))


def pack(plan, amps, targets, stage, sem):
    total = plan[2, 0]

    def tile_in(slot, place):
        row = pl.ds(pl.multiple_of(plan[0, slot] * TILE, TILE), TILE)
        column = pl.ds(pl.multiple_of(plan[1, slot] * TILE, TILE), TILE)
        return pltpu.make_async_copy(amps.at[0, row, column], stage.at[place], sem.at[0])

    def group_out(buf, group, place):
        return pltpu.make_async_copy(
            stage.at[pl.ds(place + group * GROUP, GROUP)], buf.at[pl.ds(group * GROUP, GROUP)], sem.at[1]
        )

    places = []
    place = 0
    for buf, start, stop in targets:
        end = jnp.clip(total, start, stop)

        def one(slot, carry, place=place, start=start):
            tile_in(slot, place + slot - start).start()
            return carry

        lax.fori_loop(start, end, one, 0)
        places.append((buf, place, end - start))
        place = place + buf.shape[0]
    for _, _, count in places:

        def landed(slot, carry):
            tile_in(0, 0).wait()
            return carry

        lax.fori_loop(0, count, landed, 0)
    groups = [(buf, place, (count + GROUP - 1) // GROUP) for buf, place, count in places]
    for buf, place, count in groups:

        def store(group, carry, buf=buf, place=place):
            group_out(buf, group, place).start()
            return carry

        lax.fori_loop(0, count, store, 0)
    for buf, place, count in groups:

        def stored(group, carry, buf=buf):
            group_out(buf, 0, 0).wait()
            return carry

        lax.fori_loop(0, count, stored, 0)


def pack_first(chunks, grain, plan, amps, after, first_buf, stage, sem):
    del after
    start = rest_of(plan[9, 0], chunks, grain)
    pack(plan, amps, [(first_buf, start, start + chunks[0])], stage, sem)


def pack_rest(chunks, grain, plan, amps, after, extra, *rest):
    del after
    bufs, (stage, sem) = rest[: len(chunks) - 1], rest[len(chunks) - 1 :]
    start = rest_of(plan[9, 0], chunks, grain)
    targets = [(extra, jnp.int32(0), start)]
    start = start + chunks[0]
    for buf, size in zip(bufs, chunks[1:]):
        targets.append((buf, start, start + size))
        start = start + size
    pack(plan, amps, targets, stage, sem)


def rest_of(most, chunks, grain):
    over = jnp.maximum(most - sum(chunks), 0)
    return (over + grain - 1) // grain * grain


def place_kernel(part, whole, held, sem):
    coming = pltpu.make_async_copy(part, held, sem.at[0])
    coming.start()
    coming.wait()
    leaving = pltpu.make_async_copy(held, whole.at[pl.ds(0, held.shape[0])], sem.at[1])
    leaving.start()
    leaving.wait()


def placed(part, size):
    in_hbm = pl.BlockSpec(memory_space=pltpu.HBM)
    return pl.pallas_call(
        place_kernel,
        out_shape=jax.ShapeDtypeStruct((size,) + part.shape[1:], part.dtype),
        in_specs=[in_hbm],
        out_specs=in_hbm,
        scratch_shapes=[pltpu.VMEM(part.shape, part.dtype), pltpu.SemaphoreType.DMA((2,))],
        compiler_params=pltpu.CompilerParams(vmem_limit_bytes=VMEM),
        name="placed",
    )(part)


def build_w(cap, live, where, labels, tiles, w, sem):
    blk = where[1]
    w[...] = jnp.zeros(w.shape, w.dtype)
    row_tiles = w.shape[0] // TILE

    def w_copy(slot, row_at, column_at):
        rows = pl.ds(pl.multiple_of(row_at * TILE, TILE), TILE)
        at = pl.ds(pl.multiple_of(column_at * TILE, TILE), TILE)
        return pltpu.make_async_copy(tiles.at[slot], w.at[rows, at], sem)

    def of_owner(owner, count):
        for position in range(cap):
            label = labels[owner, live + position]

            @pl.when(label >= 0)
            def _():
                place = by24(label)
                column = label - place * NT - blk * row_tiles
                w_copy(owner * cap + position, place, jnp.where(column < 0, column + NT, column)).start()

            count = count + (label >= 0).astype(jnp.int32)
        return count

    started = lax.fori_loop(0, labels.shape[0], of_owner, jnp.int32(0))

    def landed(index, carry):
        w_copy(0, 0, 0).wait()
        return carry

    lax.fori_loop(0, started, landed, 0)


def cycle_kernel(
    row_tiles, early, chunks, grain, stage, plan, energy, eps_row, eps_col, w,
    amps, bare, early_buf, prev_buf, this_buf, out_in, out, xl, xr, held, made, sems,
):
    del out_in
    steps = NT // STEP
    cols = STEP * TILE
    shift = rest_of(plan[9, 0], chunks, grain)
    total = plan[6, 0]

    def slot_at(column):
        return jnp.where(column >= NT, total, plan[5, jnp.minimum(column, NT - 1)])

    def complete(limit):
        def one(step, count):
            return count + (slot_at((step + 1) * STEP) <= limit).astype(jnp.int32)

        return lax.fori_loop(0, steps, one, jnp.int32(0))

    ends = [shift + sum(chunks[:index]) for index in range(len(chunks) + 1)]
    begin = jnp.int32(0) if stage == 0 else complete(ends[stage])
    end = jnp.int32(steps) if stage == len(chunks) - 1 else complete(ends[stage + 1])
    split = ends[stage]
    prev_start = 0 if stage == 0 else ends[stage - 1]

    def dense_copies(step, slot):
        at = pl.ds(pl.multiple_of(step * cols, cols), cols)
        return (
            pltpu.make_async_copy(amps.at[0, :, at], xl.at[slot], sems.at[0, slot]),
            pltpu.make_async_copy(bare.at[0, :, at], held.at[slot], sems.at[1, slot]),
        )

    def out_copy(step, slot):
        at = pl.ds(pl.multiple_of(step * cols, cols), cols)
        return pltpu.make_async_copy(made.at[slot], out.at[0, :, at], sems.at[3, slot])

    def tile_copy(source, place, at, slot):
        rows = pl.ds(pl.multiple_of(place * TILE, TILE), TILE)
        return pltpu.make_async_copy(source, xr.at[slot, rows, at * TILE : (at + 1) * TILE], sems.at[2, slot])

    def early_copy(column, at, slot):
        source = pl.ds(pl.multiple_of(column * TILE, TILE), TILE)
        return pltpu.make_async_copy(
            early_buf.at[0, :, source], xr.at[slot, :, at * TILE : (at + 1) * TILE], sems.at[2, slot]
        )

    def issue(step, slot):
        for copy in dense_copies(step, slot):
            copy.start()
        for at in range(STEP):
            column = step * STEP + at

            def tiles_in(column=column, at=at):
                lanes = slice(at * TILE, (at + 1) * TILE)
                xr[slot, :, lanes] = jnp.zeros((xr.shape[1], TILE), xr.dtype)
                low, high = slot_at(column), slot_at(column + 1)

                def from_buf(buf, base):
                    def one(index, carry):
                        tile_copy(buf.at[index - base], plan[3, index], at, slot).start()
                        return carry

                    return one

                middle = jnp.clip(split, low, high)
                lax.fori_loop(low, middle, from_buf(prev_buf, prev_start), 0)
                lax.fori_loop(middle, high, from_buf(this_buf, split), 0)

            if stage == 0 and early:
                pl.when(column < early)(lambda column=column, at=at: early_copy(column, at, slot).start())
                pl.when(column >= early)(tiles_in)
            else:
                tiles_in()

    def masked(ref, line, column, at, slot):
        for place in range(row_tiles):

            @pl.when(plan[line, place * NT + column] == 0)
            def _():
                ref[slot, place * TILE : (place + 1) * TILE, at * TILE : (at + 1) * TILE] = jnp.zeros(
                    (TILE, TILE), ref.dtype
                )

    def arrive(step, slot):
        for copy in dense_copies(step, slot):
            copy.wait()
        for at in range(STEP):
            column = step * STEP + at
            masked(xl, 7, column, at, slot)

            def tiles_wait(column=column):
                def one(index, carry):
                    tile_copy(this_buf.at[0], 0, 0, slot).wait()
                    return carry

                lax.fori_loop(slot_at(column), slot_at(column + 1), one, 0)

            def early_wait(column=column, at=at):
                early_copy(column, at, slot).wait()
                masked(xr, 8, column, at, slot)

            if stage == 0 and early:
                pl.when(column < early)(early_wait)
                pl.when(column >= early)(tiles_wait)
            else:
                tiles_wait()

    def product(step, slot):
        at = pl.ds(pl.multiple_of(step * cols, cols), cols)
        half = row_tiles * TILE

        for block in range(half // ROWS):
            rows = slice(block * ROWS, (block + 1) * ROWS)
            acc = jnp.dot(w[rows, :half], xl[slot], preferred_element_type=jnp.float32)
            acc = acc + jnp.dot(w[rows, half:], xr[slot], preferred_element_type=jnp.float32)
            denom = eps_row[rows, :] + eps_col[:, at] - energy[0]
            value = (held[slot, rows, :].astype(jnp.float32) + acc) / denom
            for part in range(ROWS // TILE):
                place = block * (ROWS // TILE) + part
                for column in range(STEP):
                    kept = plan[7, place * NT + step * STEP + column].astype(jnp.float32)
                    lanes = slice(column * TILE, (column + 1) * TILE)
                    piece = value[part * TILE : (part + 1) * TILE, lanes] * kept
                    made[slot, place * TILE : (place + 1) * TILE, lanes] = piece.astype(made.dtype)

    @pl.when(begin < end)
    def _():
        issue(begin, lax.rem(begin, 2))

        def one(step, carry):
            slot = lax.rem(step, 2)

            @pl.when(step + 1 < end)
            def _():
                issue(step + 1, 1 - slot)

            arrive(step, slot)

            @pl.when(step >= begin + 2)
            def _():
                out_copy(step - 2, slot).wait()

            product(step, slot)
            out_copy(step, slot).start()
            return carry

        lax.fori_loop(begin, end, one, 0)

        @pl.when(end >= begin + 2)
        def _():
            out_copy(end - 2, lax.rem(end, 2)).wait()

        out_copy(end - 1, lax.rem(end - 1, 2)).wait()


def screened_exchange(amplitudes, amp_mask, bare_ints, int_tiles, tile_ids, eps_virt, eps_pair):
    pairs, panel_rows, width = amplitudes.shape
    row_tiles = panel_rows // TILE
    cap = tile_ids.shape[2]
    owners = lax.axis_size("own")
    own, blk = lax.axis_index("own"), lax.axis_index("blk")
    where = jnp.stack([own, blk]).astype(jnp.int32)
    early, chunks, grain = EARLY, CHUNKS, GRAIN
    most_extra = row_tiles * (NT - early) - sum(chunks)
    branches = -(-most_extra // grain)
    any_space = pl.BlockSpec(memory_space=pl.ANY)
    in_hbm = pl.BlockSpec(memory_space=pltpu.HBM)
    smem = pl.BlockSpec(memory_space=pltpu.SMEM)
    vmem = pl.BlockSpec(memory_space=pltpu.VMEM)

    early_buf = passed_along(amplitudes[:, :, : early * TILE], "blk", 1)
    tiles = lax.all_gather(int_tiles, "own", axis=1, tiled=True).reshape(-1, TILE, TILE)

    live = row_tiles * NT
    wide = -(-(live + cap) // TILE) * TILE
    told = jnp.concatenate([amp_mask.reshape(1, -1), tile_ids.reshape(1, -1)], axis=1)
    told = jnp.pad(told, ((0, 0), (0, wide - live - cap)), constant_values=-1)
    told = jnp.broadcast_to(told, (2 * owners, wide))
    info = lax.all_to_all(told, ("blk", "own"), 0, 0, tiled=True).reshape(2, owners, wide)

    tile_type = lambda count: jax.ShapeDtypeStruct((count, TILE, TILE), amplitudes.dtype)
    params = pltpu.CompilerParams(vmem_limit_bytes=VMEM)
    most = branches * grain
    light = pl.CostEstimate(flops=1, bytes_accessed=1, transcendentals=0)
    plan = pl.pallas_call(
        functools.partial(make_plan, row_tiles, cap, early),
        out_shape=jax.ShapeDtypeStruct((16, wide), jnp.int32),
        in_specs=[smem, vmem],
        out_specs=vmem,
        compiler_params=params,
        cost_estimate=light,
        name="make_plan",
    )(where, info)

    def packed(kernel, sizes, after, name):
        return pl.pallas_call(
            functools.partial(kernel, chunks, grain),
            out_shape=[tile_type(size) for size in sizes],
            in_specs=[smem, in_hbm, any_space],
            out_specs=[in_hbm] * len(sizes),
            scratch_shapes=[
                pltpu.VMEM((sum(sizes), TILE, TILE), amplitudes.dtype),
                pltpu.SemaphoreType.DMA((2,)),
            ],
            compiler_params=params,
            cost_estimate=light,
            name=name,
        )(plan, amplitudes, after)

    (first,) = packed(pack_first, chunks[:1], early_buf, "pack_first")
    extra, *others = packed(pack_rest, (most,) + chunks[1:], early_buf, "pack_rest")

    def branch(index):
        def send(buf):
            if index == 0:
                return buf
            return placed(passed_along(buf[: index * grain], "blk", 1), buf.shape[0])

        return send

    shift = rest_of(plan[9, 0], chunks, grain)
    bufs = [passed_along(first, "blk", 1)]
    got = lax.switch(shift // grain, [branch(index) for index in range(branches + 1)], extra)
    got, second = lax.optimization_barrier((got, others[0]))
    bufs.append(passed_along(second, "blk", 1))
    got, tiles = lax.optimization_barrier((got, tiles))
    labels = lax.dynamic_index_in_dim(info, blk, 0, keepdims=False)
    w = pl.pallas_call(
        functools.partial(build_w, cap, live),
        out_shape=jax.ShapeDtypeStruct((panel_rows, width), jnp.bfloat16),
        in_specs=[smem, smem, any_space],
        out_specs=vmem,
        scratch_shapes=[pltpu.SemaphoreType.DMA],
        compiler_params=pltpu.CompilerParams(vmem_limit_bytes=VMEM_CYCLE),
        name="build_w",
    )(where, labels, tiles)
    w, *others = lax.optimization_barrier((w, *others[1:]))
    bufs = bufs + [passed_along(buf, "blk", 1) for buf in others]
    eps_row = lax.dynamic_slice_in_dim(eps_virt, blk * panel_rows, panel_rows, 0).reshape(panel_rows, 1)
    eps_col = eps_virt.reshape(1, width)
    cols = STEP * TILE
    out = None
    for stage in range(len(chunks)):
        prev_buf = got if stage == 0 else bufs[stage - 1]
        operands = [
            plan, eps_pair, eps_row, eps_col, w, amplitudes, bare_ints, early_buf,
            prev_buf, bufs[stage], bare_ints if out is None else out,
        ]
        out = pl.pallas_call(
            functools.partial(cycle_kernel, row_tiles, early, chunks, grain, stage),
            out_shape=jax.ShapeDtypeStruct(amplitudes.shape, amplitudes.dtype),
            in_specs=[smem, smem, vmem, vmem, vmem, in_hbm, in_hbm] + [any_space] * 3 + [in_hbm],
            out_specs=in_hbm,
            input_output_aliases={} if out is None else {10: 0},
            scratch_shapes=[pltpu.VMEM((2, panel_rows, cols), jnp.bfloat16)] * 4
            + [pltpu.SemaphoreType.DMA((4, 2))],
            compiler_params=pltpu.CompilerParams(vmem_limit_bytes=VMEM_CYCLE),
            cost_estimate=pl.CostEstimate(
                flops=2 * panel_rows * width * width // len(chunks),
                bytes_accessed=4 * panel_rows * width * 2 // len(chunks),
                transcendentals=0,
            ),
            name=f"cycle_{stage}",
        )(*operands)
    return out


def ring_exchange(amplitudes, amp_mask, bare_ints, int_tiles, tile_ids, eps_virt, eps_pair):
    pairs, panel_rows, width = amplitudes.shape
    row_tiles = panel_rows // TILE
    slots = row_tiles * NT
    mask_cells = jnp.broadcast_to(
        amp_mask.astype(jnp.bfloat16)[:, :, None, :, None], (pairs, row_tiles, TILE, NT, TILE)
    ).reshape(pairs, panel_rows, width)
    screened = amplitudes * mask_cells
    tiles = lax.all_gather(int_tiles, "own", axis=1, tiled=True)
    labels = lax.all_gather(tile_ids, "own", axis=1, tiled=True)
    flat_labels = labels.reshape(-1)
    flat_tiles = tiles.reshape(-1, TILE, TILE)
    onehot = (flat_labels[:, None] == jnp.arange(slots, dtype=jnp.int32)[None, :]).astype(jnp.bfloat16)
    grid = jnp.einsum("sq,sij->qij", onehot, flat_tiles, preferred_element_type=jnp.float32)
    w_rows = (
        grid.astype(jnp.bfloat16)
        .reshape(row_tiles, NT, TILE, TILE)
        .transpose(0, 2, 1, 3)
        .reshape(panel_rows, width)
    )
    position = lax.axis_index("blk")
    stops = lax.axis_size("blk")
    panel = screened
    cycle_sum = jnp.zeros((pairs, panel_rows, width), jnp.float32)
    for stop in range(stops):
        columns = lax.dynamic_slice_in_dim(w_rows, (position - stop) % stops * panel_rows, panel_rows, 1)
        cycle_sum = cycle_sum + jnp.einsum("ac,pcb->pab", columns, panel, preferred_element_type=jnp.float32)
        if stop + 1 < stops:
            panel = passed_along(panel, "blk", 1)
    rows_energy = lax.dynamic_slice_in_dim(eps_virt, position * panel_rows, panel_rows, 0)
    denom = rows_energy[None, :, None] + eps_virt[None, None, :] - eps_pair[:, None, None]
    updated = (bare_ints.astype(jnp.float32) + cycle_sum) / denom * mask_cells.astype(jnp.float32)
    return updated.astype(jnp.bfloat16)


def solution(mesh):
    local = screened_exchange if mesh.shape["blk"] == 2 else ring_exchange
    in_specs = (
        P("own", "blk", None),
        P("own", "blk", None),
        P("own", "blk", None),
        P("blk", "own", None, None, None),
        P("blk", "own", None),
        P(),
        P("own"),
    )
    out_specs = P("own", "blk", None)
    return jax.shard_map(local, mesh=mesh, in_specs=in_specs, out_specs=out_specs, check_vma=False)
```

```python
import functools

import jax
import jax.numpy as jnp
from jax import lax
from jax.experimental import pallas as pl
from jax.experimental.pallas import tpu as pltpu
from jax.sharding import PartitionSpec as P

TILE = 128
NT = 24
STEP = 2
EARLY = 24
CHUNKS = (40, 40, 24)
SIZES = (0, 16, 24, 32, 40, 48, 56, 64, 72, 88, 112)
PAIR = 2
DEPTHS = (3, 4, 5, 6)
GROUP = 8
VMEM = 62 * 1024 * 1024
VMEM_CYCLE = 40 * 1024 * 1024


def passed_along(value, axis, steps):
    count = lax.axis_size(axis)
    pairs = [(source, (source + steps) % count) for source in range(count)]
    return lax.ppermute(value, axis, pairs)


def by24(index):
    return (index * 2731) >> 16


def plan_and_pack(
    row_tiles, cap, early, chunks, sizes, where, info, amps, after, plan_out, first_buf, plan, plan_sem, stage, sem
):
    del after
    width = info.shape[1] // 2
    live = row_tiles * NT
    own, blk = where[0], where[1]
    infos = [info[:, :width], info[:, width:]]
    row = lax.broadcasted_iota(jnp.int32, (width, width), 0)
    lane = lax.broadcasted_iota(jnp.int32, (width, width), 1)
    row_hi, lane_hi = by24(row), by24(lane)
    row_lo, lane_lo = row - row_hi * NT, lane - lane_hi * NT
    same_lo = (row_lo == lane_lo).astype(jnp.float32)
    row_key, lane_key = row_lo * row_tiles + row_hi, lane_lo * row_tiles + lane_hi
    ahead = ((row_key < lane_key) & (row < live)).astype(jnp.bfloat16)
    places = lax.broadcasted_iota(jnp.int32, (8, width), 1)
    places_hi = by24(places)
    which = lax.broadcasted_iota(jnp.int32, (8, width), 0)
    digits = jnp.where(which == 0, places_hi, jnp.where(which == 1, places - places_hi * NT, 0))
    digits = digits.astype(jnp.bfloat16)
    owners = info.shape[0]
    mine = (lax.broadcasted_iota(jnp.int32, (owners, 1), 0) == own).astype(jnp.float32)
    lanes = lax.broadcasted_iota(jnp.int32, (owners, width), 1)

    def before(flags):
        return jnp.dot(flags.astype(jnp.bfloat16), ahead, preferred_element_type=jnp.float32)

    def listed(flags, count_before):
        count_column = jnp.sum(jnp.where(row == lane, count_before, 0.0), axis=1, keepdims=True)
        flag_column = jnp.sum(jnp.where(row == lane, flags, 0.0), axis=1, keepdims=True)
        onehot = jnp.where(count_column == lane.astype(jnp.float32), flag_column, 0.0)
        return jnp.dot(digits, onehot.astype(jnp.bfloat16), preferred_element_type=jnp.float32)

    def my_row(rows):
        return jnp.sum(rows * mine, axis=0, keepdims=True)

    most = jnp.int32(0)
    found = []
    for g in range(2):
        h = 1 - g
        seen = jnp.zeros((owners, width), jnp.float32)
        for slot in range(cap):
            seen = seen + (infos[g][:, live + slot : live + slot + 1] == lanes).astype(jnp.float32)
        seen = jnp.sum(seen, axis=0, keepdims=True)
        left = jnp.where(row_hi == lane_hi, seen, 0.0).astype(jnp.bfloat16)
        sender = 1 - blk if g == 0 else blk
        right = (row_lo == sender * row_tiles + lane_hi).astype(jnp.bfloat16)
        meets = jnp.dot(left, right, preferred_element_type=jnp.float32) * same_lo
        kept_rows = jnp.where(lanes < live, infos[g], 0).astype(jnp.bfloat16)
        hits = jnp.dot(kept_rows, meets.astype(jnp.bfloat16), preferred_element_type=jnp.float32)
        kept_columns = jnp.where(lanes < live, infos[h], 0)
        need = jnp.where((hits > 0.5) & (kept_columns > 0), 1.0, 0.0)
        kept = kept_columns.astype(jnp.float32)
        kept_before = before(kept)
        late = jnp.where(kept_before >= early, need, 0.0)
        count = jnp.sum(late, axis=1, keepdims=True)
        most = jnp.maximum(most, jnp.max(count * mine).astype(jnp.int32))
        my_late = my_row(late)
        my_count = jnp.sum(my_late, axis=1, keepdims=True)
        late_before = before(my_late)
        late_list = listed(my_late, late_before)
        found.append((late_list[0:1], late_list[1:2], late_before, jnp.broadcast_to(my_count, (1, width))))
        if g == 0:
            my_kept, my_kept_before = my_row(kept), my_row(kept_before)
            early_list = listed(my_kept, my_kept_before)
            early_lines = [early_list[0:1], early_list[1:2], my_kept_before]
            my_total = jnp.broadcast_to(jnp.sum(my_kept, axis=1, keepdims=True), (1, width))
    own_mask = my_row(jnp.where(lanes < live, infos[0], 0).astype(jnp.float32))
    received, sent = found
    lines = [
        sent[0], sent[1], sent[3], received[0], received[1], received[2], received[3], own_mask,
    ] + early_lines
    for index, line in enumerate(lines):
        plan_out[index : index + 1, :] = line.astype(jnp.int32)
    plan_out[11:12, :] = jnp.broadcast_to(most, (1, width))
    plan_out[12:13, :] = my_total.astype(jnp.int32)
    copy = pltpu.make_async_copy(plan_out, plan, plan_sem)
    copy.start()
    copy.wait()
    start = rest_of(plan[11, 0], chunks, sizes)
    pack(plan, amps, [(first_buf, start, start + chunks[0])], stage, sem)


def pack(plan, amps, targets, stage, sem):
    total = plan[2, 0]

    def tile_in(slot, place):
        row = pl.ds(pl.multiple_of(plan[0, slot] * TILE, TILE), TILE)
        column = pl.ds(pl.multiple_of(plan[1, slot] * TILE, TILE), TILE)
        return pltpu.make_async_copy(amps.at[0, row, column], stage.at[place], sem.at[0])

    def group_out(buf, group, place):
        return pltpu.make_async_copy(
            stage.at[pl.ds(place + group * GROUP, GROUP)], buf.at[pl.ds(group * GROUP, GROUP)], sem.at[1]
        )

    places = []
    place = 0
    for buf, start, stop in targets:
        end = jnp.clip(total, start, stop)

        def one(slot, carry, place=place, start=start):
            tile_in(slot, place + slot - start).start()
            return carry

        lax.fori_loop(start, end, one, 0)
        places.append((buf, place, end - start))
        place = place + buf.shape[0]
    for _, _, count in places:

        def landed(slot, carry):
            tile_in(0, 0).wait()
            return carry

        lax.fori_loop(0, count, landed, 0)
    groups = [(buf, place, (count + GROUP - 1) // GROUP) for buf, place, count in places]
    for buf, place, count in groups:

        def store(group, carry, buf=buf, place=place):
            group_out(buf, group, place).start()
            return carry

        lax.fori_loop(0, count, store, 0)
    for buf, place, count in groups:

        def stored(group, carry, buf=buf):
            group_out(buf, 0, 0).wait()
            return carry

        lax.fori_loop(0, count, stored, 0)


def pack_early(row_tiles, mask, amps, buf, stage, sem):
    count = buf.shape[0]

    def tile_in(place, column, at):
        rows = pl.ds(pl.multiple_of(place * TILE, TILE), TILE)
        lanes = pl.ds(pl.multiple_of(column * TILE, TILE), TILE)
        return pltpu.make_async_copy(amps.at[0, rows, lanes], stage.at[at], sem.at[0])

    def one_column(state):
        column, found = state
        for place in range(row_tiles):
            kept = (mask[0, place, column] > 0) & (found < count)
            pl.when(kept)(lambda place=place, found=found: tile_in(place, column, found).start())
            found = found + kept.astype(jnp.int32)
        return column + 1, found

    _, found = lax.while_loop(
        lambda state: (state[0] < NT) & (state[1] < count), one_column, (jnp.int32(0), jnp.int32(0))
    )

    def landed(index, carry):
        tile_in(0, 0, 0).wait()
        return carry

    lax.fori_loop(0, found, landed, 0)
    leaving = pltpu.make_async_copy(stage, buf, sem.at[1])
    leaving.start()
    leaving.wait()


def pack_rest(chunks, sizes, plan, amps, *rest):
    extra, *bufs = rest[-2 - len(chunks) : -2]
    stage, sem = rest[-2:]
    start = rest_of(plan[11, 0], chunks, sizes)
    targets = [(extra, jnp.int32(0), start)]
    start = start + chunks[0]
    for buf, size in zip(bufs, chunks[1:]):
        targets.append((buf, start, start + size))
        start = start + size
    pack(plan, amps, targets, stage, sem)


def extra_sizes(most):
    return [size for size in SIZES if size < most] + [most]


def rest_of(most, chunks, sizes):
    over = most - sum(chunks)
    size = jnp.int32(sizes[0])
    for low, high in zip(sizes, sizes[1:]):
        size = jnp.where(over > low, high, size)
    return size


def place_kernel(part, whole, held, sem):
    coming = pltpu.make_async_copy(part, held, sem.at[0])
    coming.start()
    coming.wait()
    leaving = pltpu.make_async_copy(held, whole.at[pl.ds(0, held.shape[0])], sem.at[1])
    leaving.start()
    leaving.wait()


def placed(part, size):
    any_space = pl.BlockSpec(memory_space=pl.ANY)
    return pl.pallas_call(
        place_kernel,
        out_shape=jax.ShapeDtypeStruct((size,) + part.shape[1:], part.dtype),
        in_specs=[any_space],
        out_specs=any_space,
        scratch_shapes=[pltpu.VMEM(part.shape, part.dtype), pltpu.SemaphoreType.DMA((2,))],
        compiler_params=pltpu.CompilerParams(vmem_limit_bytes=VMEM),
        name="placed",
    )(part)


def depth_for(pairs):
    depths = [depth for depth in DEPTHS if depth < NT // 2] + [NT // 2]
    wanted = jnp.int32(depths[0])
    for low, high in zip(depths, depths[1:]):
        wanted = jnp.where(pairs > low, high, wanted)
    return wanted, depths


def build_w(cap, live, where, labels, tiles, w_out, table, w, found, counts, listed, sem):
    blk = where[1]
    row_tiles = w.shape[0] // TILE
    blocks = row_tiles // PAIR

    def clear(block, carry):
        counts[block] = 0
        for column in range(NT):
            found[block, column] = -1
            table[block, column] = 0
        return carry

    lax.fori_loop(0, blocks, clear, 0)

    def of_owner(owner, count):
        for position in range(cap):
            label = labels[owner, live + position]

            @pl.when(label >= 0)
            def _(count=count):
                place = by24(label)
                column = label - place * NT - blk * row_tiles
                column = jnp.where(column < 0, column + NT, column)
                block = lax.shift_right_logical(place, 1)
                held = found[block, column]
                known = counts[block]
                at = jnp.where(held < 0, known, held)
                found[block, column] = at
                counts[block] = jnp.where(held < 0, known + 1, known)
                table[block, at] = column
                listed[0, count] = owner * cap + position
                listed[1, count] = place
                listed[2, count] = at

            count = count + (label >= 0).astype(jnp.int32)
        return count

    total = lax.fori_loop(0, labels.shape[0], of_owner, jnp.int32(0))
    pairs = lax.fori_loop(
        0, blocks, lambda block, most: jnp.maximum(most, (counts[block] + 1) // 2), jnp.int32(1)
    )
    table[blocks, 0] = pairs
    wanted, _ = depth_for(pairs)

    def zero(pair, carry):
        at = pl.ds(pl.multiple_of(pair * 2 * TILE, 2 * TILE), 2 * TILE)
        w[:, at] = jnp.zeros((w.shape[0], 2 * TILE), w.dtype)
        return carry

    lax.fori_loop(0, wanted, zero, 0)

    def tile_in(index):
        rows = pl.ds(pl.multiple_of(listed[1, index] * TILE, TILE), TILE)
        at = pl.ds(pl.multiple_of(listed[2, index] * TILE, TILE), TILE)
        return pltpu.make_async_copy(tiles.at[listed[0, index]], w.at[rows, at], sem.at[0])

    def start_in(index, carry):
        tile_in(index).start()
        return carry

    def landed(index, carry):
        tile_in(0).wait()
        return carry

    lax.fori_loop(0, total, start_in, 0)
    lax.fori_loop(0, total, landed, 0)

    def pair_out(pair):
        at = pl.ds(pl.multiple_of(pair * 2 * TILE, 2 * TILE), 2 * TILE)
        return pltpu.make_async_copy(w.at[:, at], w_out.at[:, at], sem.at[1])

    def start_out(pair, carry):
        pair_out(pair).start()
        return carry

    def left(pair, carry):
        pair_out(pair).wait()
        return carry

    lax.fori_loop(0, wanted, start_out, 0)
    lax.fori_loop(0, wanted, left, 0)


def cycle_kernel(
    row_tiles, early, chunks, sizes, stage, plan, table, energy, eps_row, eps_col, w_in,
    amps, bare, early_buf, prev_buf, this_buf, out_in, out, w, x, held, made, sems, w_sem,
):
    del out_in
    half = row_tiles * TILE
    pairs = table[row_tiles // PAIR, 0]
    steps = NT // STEP
    cols = STEP * TILE
    shift = rest_of(plan[11, 0], chunks, sizes)
    total = plan[6, 0]

    def slot_at(column):
        return jnp.where(column >= NT, total, plan[5, jnp.minimum(column, NT - 1)])

    def complete(limit):
        def one(step, count):
            return count + (slot_at((step + 1) * STEP) <= limit).astype(jnp.int32)

        return lax.fori_loop(0, steps, one, jnp.int32(0))

    ends = [shift + sum(chunks[:index]) for index in range(len(chunks) + 1)]
    begin = jnp.int32(0) if stage == 0 else complete(ends[stage])
    end = jnp.int32(steps) if stage == len(chunks) - 1 else complete(ends[stage + 1])
    split = ends[stage]
    prev_start = 0 if stage == 0 else ends[stage - 1]

    def dense_copies(step, slot):
        at = pl.ds(pl.multiple_of(step * cols, cols), cols)
        return (
            pltpu.make_async_copy(amps.at[0, :, at], x.at[slot, :half], sems.at[0, slot]),
            pltpu.make_async_copy(bare.at[0, :, at], held.at[slot], sems.at[1, slot]),
        )

    def out_copy(step, slot):
        at = pl.ds(pl.multiple_of(step * cols, cols), cols)
        return pltpu.make_async_copy(made.at[slot], out.at[0, :, at], sems.at[3, slot])

    def tile_copy(source, place, at, slot):
        rows = pl.ds(pl.multiple_of(half + place * TILE, TILE), TILE)
        return pltpu.make_async_copy(source, x.at[slot, rows, at * TILE : (at + 1) * TILE], sems.at[2, slot])

    def early_at(column):
        known = jnp.where(column >= NT, plan[12, 0], plan[10, jnp.minimum(column, NT - 1)])
        return jnp.minimum(known, early)

    def issue(step, slot):
        for copy in dense_copies(step, slot):
            copy.start()
        for at in range(STEP):
            column = step * STEP + at
            lanes = slice(at * TILE, (at + 1) * TILE)
            x[slot, half:, lanes] = jnp.zeros((half, TILE), x.dtype)
            low, high = slot_at(column), slot_at(column + 1)
            middle = jnp.clip(split, low, high)

            def from_buf(buf, base, line, at=at):
                def one(index, carry):
                    tile_copy(buf.at[index - base], plan[line, index], at, slot).start()
                    return carry

                return one

            lax.fori_loop(early_at(column), early_at(column + 1), from_buf(early_buf, 0, 8), 0)
            lax.fori_loop(low, middle, from_buf(prev_buf, prev_start, 3), 0)
            lax.fori_loop(middle, high, from_buf(this_buf, split, 3), 0)

    def masked(base, line, column, at, slot):
        for place in range(row_tiles):

            @pl.when(plan[line, place * NT + column] == 0)
            def _():
                rows = slice(base + place * TILE, base + (place + 1) * TILE)
                x[slot, rows, at * TILE : (at + 1) * TILE] = jnp.zeros((TILE, TILE), x.dtype)

    def arrive(step, slot):
        for copy in dense_copies(step, slot):
            copy.wait()
        for at in range(STEP):
            masked(0, 7, step * STEP + at, at, slot)

        def landed(index, carry):
            tile_copy(this_buf.at[0], 0, 0, slot).wait()
            return carry

        first, last = step * STEP, (step + 1) * STEP
        lax.fori_loop(0, early_at(last) - early_at(first) + slot_at(last) - slot_at(first), landed, 0)

    def product(step, slot, depth):
        at = pl.ds(pl.multiple_of(step * cols, cols), cols)
        for block in range(row_tiles // PAIR):
            rows = slice(block * PAIR * TILE, (block + 1) * PAIR * TILE)
            acc = None
            for pair in range(depth):
                pieces = []
                for index in (2 * pair, 2 * pair + 1):
                    place = pl.multiple_of(table[block, index] * TILE, TILE)
                    pieces.append(x[slot, pl.ds(place, TILE), :])
                part = jnp.dot(
                    w[rows, pair * 2 * TILE : (pair + 1) * 2 * TILE],
                    jnp.concatenate(pieces, axis=0),
                    preferred_element_type=jnp.float32,
                )
                acc = part if acc is None else acc + part
            denom = eps_row[rows, :] + eps_col[:, at] - energy[0]
            value = (held[slot, rows, :].astype(jnp.float32) + acc) / denom
            for part in range(PAIR):
                place = block * PAIR + part
                for column in range(STEP):
                    kept = plan[7, place * NT + step * STEP + column].astype(jnp.float32)
                    lanes = slice(column * TILE, (column + 1) * TILE)
                    piece = value[part * TILE : (part + 1) * TILE, lanes] * kept
                    made[slot, place * TILE : (place + 1) * TILE, lanes] = piece.astype(made.dtype)

    def w_copy(pair):
        at = pl.ds(pl.multiple_of(pair * 2 * TILE, 2 * TILE), 2 * TILE)
        return pltpu.make_async_copy(w_in.at[:, at], w.at[:, at], w_sem)

    @pl.when(begin < end)
    def _():
        wanted, depths = depth_for(pairs)

        def load(pair, carry):
            w_copy(pair).start()
            return carry

        lax.fori_loop(0, wanted, load, 0)
        issue(begin, lax.rem(begin, 2))

        def loaded(pair, carry):
            w_copy(pair).wait()
            return carry

        lax.fori_loop(0, wanted, loaded, 0)

        def one(step, carry):
            slot = lax.rem(step, 2)

            @pl.when(step + 1 < end)
            def _():
                issue(step + 1, 1 - slot)

            arrive(step, slot)

            @pl.when(step >= begin + 2)
            def _():
                out_copy(step - 2, slot).wait()

            for depth in depths:
                pl.when(wanted == depth)(functools.partial(product, step, slot, depth))
            out_copy(step, slot).start()
            return carry

        lax.fori_loop(begin, end, one, 0)

        @pl.when(end >= begin + 2)
        def _():
            out_copy(end - 2, lax.rem(end, 2)).wait()

        out_copy(end - 1, lax.rem(end - 1, 2)).wait()


def screened_exchange(amplitudes, amp_mask, bare_ints, int_tiles, tile_ids, eps_virt, eps_pair):
    pairs, panel_rows, width = amplitudes.shape
    row_tiles = panel_rows // TILE
    cap = tile_ids.shape[2]
    owners = lax.axis_size("own")
    own, blk = lax.axis_index("own"), lax.axis_index("blk")
    where = jnp.stack([own, blk]).astype(jnp.int32)
    early, chunks = EARLY, CHUNKS
    most_extra = row_tiles * NT - sum(chunks)
    sizes = extra_sizes(most_extra)
    any_space = pl.BlockSpec(memory_space=pl.ANY)
    in_hbm = pl.BlockSpec(memory_space=pltpu.HBM)
    smem = pl.BlockSpec(memory_space=pltpu.SMEM)
    vmem = pl.BlockSpec(memory_space=pltpu.VMEM)

    tiles = lax.all_gather(int_tiles, "own", axis=1, tiled=True).reshape(-1, TILE, TILE)

    live = row_tiles * NT
    wide = -(-(live + cap) // TILE) * TILE
    told = jnp.concatenate([amp_mask.reshape(1, -1), tile_ids.reshape(1, -1)], axis=1)
    told = jnp.pad(told, ((0, 0), (0, wide - live - cap)), constant_values=-1)
    partner_told = passed_along(told, "blk", 1)
    tile_type = lambda count: jax.ShapeDtypeStruct((count, TILE, TILE), amplitudes.dtype)
    params = pltpu.CompilerParams(vmem_limit_bytes=VMEM)
    light = pl.CostEstimate(flops=1, bytes_accessed=1, transcendentals=0)
    early_tiles = pl.pallas_call(
        functools.partial(pack_early, row_tiles),
        out_shape=tile_type(early),
        in_specs=[smem, in_hbm],
        out_specs=in_hbm,
        scratch_shapes=[pltpu.VMEM((early, TILE, TILE), amplitudes.dtype), pltpu.SemaphoreType.DMA((2,))],
        compiler_params=params,
        cost_estimate=light,
        name="pack_early",
    )(amp_mask, amplitudes)
    partner_told, early_tiles = lax.optimization_barrier((partner_told, early_tiles))
    early_buf = passed_along(early_tiles, "blk", 1)
    told = jnp.broadcast_to(jnp.concatenate([told, partner_told], axis=1), (owners, 2 * wide))
    info = lax.all_to_all(told, "own", 0, 0, tiled=True)

    most = most_extra
    plan, first = pl.pallas_call(
        functools.partial(plan_and_pack, row_tiles, cap, early, chunks, sizes),
        out_shape=[jax.ShapeDtypeStruct((16, wide), jnp.int32), tile_type(chunks[0])],
        in_specs=[smem, vmem, in_hbm, any_space],
        out_specs=[vmem, in_hbm],
        scratch_shapes=[
            pltpu.SMEM((16, wide), jnp.int32),
            pltpu.SemaphoreType.DMA,
            pltpu.VMEM((chunks[0], TILE, TILE), amplitudes.dtype),
            pltpu.SemaphoreType.DMA((2,)),
        ],
        compiler_params=params,
        cost_estimate=light,
        name="plan_and_pack",
    )(where, info, amplitudes, early_buf)
    counts = (most,) + chunks[1:]
    extra, *others = pl.pallas_call(
        functools.partial(pack_rest, chunks, sizes),
        out_shape=[tile_type(size) for size in counts],
        in_specs=[smem, in_hbm],
        out_specs=[in_hbm] * len(counts),
        scratch_shapes=[
            pltpu.VMEM((sum(counts), TILE, TILE), amplitudes.dtype),
            pltpu.SemaphoreType.DMA((2,)),
        ],
        compiler_params=params,
        cost_estimate=light,
        name="pack_rest",
    )(plan, amplitudes)

    def branch(size):
        def send(buf):
            if size == 0:
                return buf
            return placed(passed_along(buf[:size], "blk", 1), buf.shape[0])

        return send

    place = sum((plan[11, 0] - sum(chunks) > size).astype(jnp.int32) for size in sizes[:-1])
    bufs = [passed_along(first, "blk", 1)]
    got = lax.switch(place, [branch(size) for size in sizes], extra)
    got, second = lax.optimization_barrier((got, others[0]))
    bufs.append(passed_along(second, "blk", 1))
    got, tiles = lax.optimization_barrier((got, tiles))
    labels = info[:, :wide]
    blocks = row_tiles // PAIR
    w, table = pl.pallas_call(
        functools.partial(build_w, cap, live),
        out_shape=[
            jax.ShapeDtypeStruct((panel_rows, width), jnp.bfloat16),
            jax.ShapeDtypeStruct((blocks + 1, NT), jnp.int32),
        ],
        in_specs=[smem, smem, any_space],
        out_specs=[in_hbm, smem],
        scratch_shapes=[
            pltpu.VMEM((panel_rows, width), jnp.bfloat16),
            pltpu.SMEM((blocks, NT), jnp.int32),
            pltpu.SMEM((blocks,), jnp.int32),
            pltpu.SMEM((3, owners * cap), jnp.int32),
            pltpu.SemaphoreType.DMA((2,)),
        ],
        compiler_params=pltpu.CompilerParams(vmem_limit_bytes=VMEM_CYCLE),
        name="build_w",
    )(where, labels, tiles)
    w, *others = lax.optimization_barrier((w, *others[1:]))
    bufs = bufs + [passed_along(buf, "blk", 1) for buf in others]
    eps_row = lax.dynamic_slice_in_dim(eps_virt, blk * panel_rows, panel_rows, 0).reshape(panel_rows, 1)
    eps_col = eps_virt.reshape(1, width)
    cols = STEP * TILE
    out = None
    for stage in range(len(chunks)):
        prev_buf = got if stage == 0 else bufs[stage - 1]
        operands = [
            plan, table, eps_pair, eps_row, eps_col, w, amplitudes, bare_ints, early_buf,
            prev_buf, bufs[stage], bare_ints if out is None else out,
        ]
        out = pl.pallas_call(
            functools.partial(cycle_kernel, row_tiles, early, chunks, sizes, stage),
            out_shape=jax.ShapeDtypeStruct(amplitudes.shape, amplitudes.dtype),
            in_specs=[smem] * 3 + [vmem] * 2 + [any_space] + [in_hbm] * 2 + [any_space] * 3 + [in_hbm],
            out_specs=in_hbm,
            input_output_aliases={} if out is None else {11: 0},
            scratch_shapes=[
                pltpu.VMEM((panel_rows, width), jnp.bfloat16),
                pltpu.VMEM((2, width, cols), jnp.bfloat16),
                pltpu.VMEM((2, panel_rows, cols), jnp.bfloat16),
                pltpu.VMEM((2, panel_rows, cols), jnp.bfloat16),
                pltpu.SemaphoreType.DMA((4, 2)),
                pltpu.SemaphoreType.DMA,
            ],
            compiler_params=pltpu.CompilerParams(vmem_limit_bytes=VMEM_CYCLE),
            cost_estimate=pl.CostEstimate(
                flops=2 * panel_rows * width * width // len(chunks),
                bytes_accessed=4 * panel_rows * width * 2 // len(chunks),
                transcendentals=0,
            ),
            name=f"cycle_{stage}",
        )(*operands)
    return out


def ring_exchange(amplitudes, amp_mask, bare_ints, int_tiles, tile_ids, eps_virt, eps_pair):
    pairs, panel_rows, width = amplitudes.shape
    row_tiles = panel_rows // TILE
    slots = row_tiles * NT
    mask_cells = jnp.broadcast_to(
        amp_mask.astype(jnp.bfloat16)[:, :, None, :, None], (pairs, row_tiles, TILE, NT, TILE)
    ).reshape(pairs, panel_rows, width)
    screened = amplitudes * mask_cells
    tiles = lax.all_gather(int_tiles, "own", axis=1, tiled=True)
    labels = lax.all_gather(tile_ids, "own", axis=1, tiled=True)
    flat_labels = labels.reshape(-1)
    flat_tiles = tiles.reshape(-1, TILE, TILE)
    onehot = (flat_labels[:, None] == jnp.arange(slots, dtype=jnp.int32)[None, :]).astype(jnp.bfloat16)
    grid = jnp.einsum("sq,sij->qij", onehot, flat_tiles, preferred_element_type=jnp.float32)
    w_rows = (
        grid.astype(jnp.bfloat16)
        .reshape(row_tiles, NT, TILE, TILE)
        .transpose(0, 2, 1, 3)
        .reshape(panel_rows, width)
    )
    position = lax.axis_index("blk")
    stops = lax.axis_size("blk")
    panel = screened
    cycle_sum = jnp.zeros((pairs, panel_rows, width), jnp.float32)
    for stop in range(stops):
        columns = lax.dynamic_slice_in_dim(w_rows, (position - stop) % stops * panel_rows, panel_rows, 1)
        cycle_sum = cycle_sum + jnp.einsum("ac,pcb->pab", columns, panel, preferred_element_type=jnp.float32)
        if stop + 1 < stops:
            panel = passed_along(panel, "blk", 1)
    rows_energy = lax.dynamic_slice_in_dim(eps_virt, position * panel_rows, panel_rows, 0)
    denom = rows_energy[None, :, None] + eps_virt[None, None, :] - eps_pair[:, None, None]
    updated = (bare_ints.astype(jnp.float32) + cycle_sum) / denom * mask_cells.astype(jnp.float32)
    return updated.astype(jnp.bfloat16)


def solution(mesh):
    local = screened_exchange if mesh.shape["blk"] == 2 else ring_exchange
    in_specs = (
        P("own", "blk", None),
        P("own", "blk", None),
        P("own", "blk", None),
        P("blk", "own", None, None, None),
        P("blk", "own", None),
        P(),
        P("own"),
    )
    out_specs = P("own", "blk", None)
    return jax.shard_map(local, mesh=mesh, in_specs=in_specs, out_specs=out_specs, check_vma=False)
```

```python
import functools

import jax
import jax.numpy as jnp
from jax import lax
from jax.experimental import pallas as pl
from jax.experimental.pallas import tpu as pltpu
from jax.sharding import PartitionSpec as P

TILE = 128
NT = 24
STEP = 2
EARLY = 28
CHUNKS = (48, 40, 16)
SIZES = (8, 16, 24, 32, 40, 48, 56, 64, 80)
PAIR = 2
DEPTHS = (3, 4, 5, 6)
GROUP = 8
VMEM = 55 * 1024 * 1024


def passed_along(value, axis, steps):
    count = lax.axis_size(axis)
    pairs = [(source, (source + steps) % count) for source in range(count)]
    return lax.ppermute(value, axis, pairs)


def by24(index):
    return (index * 2731) >> 16


def make_plan(row_tiles, cap, early, where, info, plan_out):
    width = info.shape[1] // 2
    live = row_tiles * NT
    own, blk = where[0], where[1]
    infos = [info[:, :width], info[:, width:]]
    row = lax.broadcasted_iota(jnp.int32, (width, width), 0)
    lane = lax.broadcasted_iota(jnp.int32, (width, width), 1)
    row_hi, lane_hi = by24(row), by24(lane)
    row_lo, lane_lo = row - row_hi * NT, lane - lane_hi * NT
    same_lo = (row_lo == lane_lo).astype(jnp.float32)
    row_key, lane_key = row_lo * row_tiles + row_hi, lane_lo * row_tiles + lane_hi
    ahead = ((row_key < lane_key) & (row < live)).astype(jnp.bfloat16)
    places = lax.broadcasted_iota(jnp.int32, (8, width), 1)
    places_hi = by24(places)
    which = lax.broadcasted_iota(jnp.int32, (8, width), 0)
    digits = jnp.where(which == 0, places_hi, jnp.where(which == 1, places - places_hi * NT, 0))
    digits = digits.astype(jnp.bfloat16)
    owners = info.shape[0]
    mine = (lax.broadcasted_iota(jnp.int32, (owners, 1), 0) == own).astype(jnp.float32)
    lanes = lax.broadcasted_iota(jnp.int32, (owners, width), 1)

    def before(flags):
        return jnp.dot(flags.astype(jnp.bfloat16), ahead, preferred_element_type=jnp.float32)

    def listed(flags, count_before):
        count_column = jnp.sum(jnp.where(row == lane, count_before, 0.0), axis=1, keepdims=True)
        flag_column = jnp.sum(jnp.where(row == lane, flags, 0.0), axis=1, keepdims=True)
        onehot = jnp.where(count_column == lane.astype(jnp.float32), flag_column, 0.0)
        return jnp.dot(digits, onehot.astype(jnp.bfloat16), preferred_element_type=jnp.float32)

    masks = [
        jnp.broadcast_to(
            jnp.sum(jnp.where(lanes < live, info, 0).astype(jnp.float32) * mine, axis=0, keepdims=True), (8, width)
        )
        for info in infos
    ]

    most = jnp.int32(0)
    found = []
    for g in range(2):
        h = 1 - g
        seen = jnp.zeros((owners, width), jnp.float32)
        for slot in range(cap):
            seen = seen + (infos[g][:, live + slot : live + slot + 1] == lanes).astype(jnp.float32)
        seen = jnp.sum(seen, axis=0, keepdims=True)
        left = jnp.where(row_hi == lane_hi, seen, 0.0).astype(jnp.bfloat16)
        sender = 1 - blk if g == 0 else blk
        right = (row_lo == sender * row_tiles + lane_hi).astype(jnp.bfloat16)
        meets = jnp.dot(left, right, preferred_element_type=jnp.float32) * same_lo
        hits = jnp.dot(masks[g].astype(jnp.bfloat16), meets.astype(jnp.bfloat16), preferred_element_type=jnp.float32)
        need = jnp.where(hits > 0.5, masks[h], 0.0)
        kept_before = before(masks[h])
        late = jnp.where(kept_before >= early, need, 0.0)
        count = jnp.sum(late, axis=1, keepdims=True)
        most = jnp.maximum(most, jnp.max(count).astype(jnp.int32))
        found.append((late, before(late), count, kept_before))

    def write(lines):
        for index, line in lines.items():
            plan_out[index : index + 1, :] = jnp.broadcast_to(line[:1].astype(jnp.int32), (1, width))

    late, late_before, count, _ = found[1]
    sent_list = listed(late[:1], late_before[:1])
    write({0: sent_list[0:1], 1: sent_list[1:2], 2: count, 7: masks[0]})
    plan_out[11:12, :] = jnp.broadcast_to(most, (1, width))
    late, late_before, count, kept_before = found[0]
    late_list = listed(late[:1], late_before[:1])
    early_list = listed(masks[1][:1], kept_before[:1])
    total = jnp.sum(masks[1], axis=1, keepdims=True)
    write({3: late_list[0:1], 4: late_list[1:2], 5: late_before, 6: count})
    write({8: early_list[0:1], 9: early_list[1:2], 10: kept_before, 12: total})


def pack(plan, amps, targets, stage, sem):
    total = plan[2, 0]

    def tile_in(slot, place):
        row = pl.ds(pl.multiple_of(plan[0, slot] * TILE, TILE), TILE)
        column = pl.ds(pl.multiple_of(plan[1, slot] * TILE, TILE), TILE)
        return pltpu.make_async_copy(amps.at[0, row, column], stage.at[place], sem.at[0])

    def group_out(buf, group, place):
        return pltpu.make_async_copy(
            stage.at[pl.ds(place + group * GROUP, GROUP)], buf.at[pl.ds(group * GROUP, GROUP)], sem.at[1]
        )

    places = []
    place = 0
    for buf, start, stop in targets:
        end = jnp.clip(total, start, stop)

        def one(slot, carry, place=place, start=start):
            tile_in(slot, place + slot - start).start()
            return carry

        lax.fori_loop(start, end, one, 0)
        places.append((buf, place, end - start))
        place = place + buf.shape[0]
    for _, _, count in places:

        def landed(slot, carry):
            tile_in(0, 0).wait()
            return carry

        lax.fori_loop(0, count, landed, 0)
    groups = [(buf, place, (count + GROUP - 1) // GROUP) for buf, place, count in places]
    for buf, place, count in groups:

        def store(group, carry, buf=buf, place=place):
            group_out(buf, group, place).start()
            return carry

        lax.fori_loop(0, count, store, 0)
    for buf, place, count in groups:

        def stored(group, carry, buf=buf):
            group_out(buf, 0, 0).wait()
            return carry

        lax.fori_loop(0, count, stored, 0)


def pack_early(row_tiles, mask, amps, buf, stage, sem):
    count = buf.shape[0]

    def tile_in(place, column, at):
        rows = pl.ds(pl.multiple_of(place * TILE, TILE), TILE)
        lanes = pl.ds(pl.multiple_of(column * TILE, TILE), TILE)
        return pltpu.make_async_copy(amps.at[0, rows, lanes], stage.at[at], sem.at[0])

    def one_column(state):
        column, found = state
        for place in range(row_tiles):
            kept = (mask[0, place, column] > 0) & (found < count)
            pl.when(kept)(lambda place=place, found=found: tile_in(place, column, found).start())
            found = found + kept.astype(jnp.int32)
        return column + 1, found

    _, found = lax.while_loop(
        lambda state: (state[0] < NT) & (state[1] < count), one_column, (jnp.int32(0), jnp.int32(0))
    )

    def landed(index, carry):
        tile_in(0, 0, 0).wait()
        return carry

    lax.fori_loop(0, found, landed, 0)
    leaving = pltpu.make_async_copy(stage, buf, sem.at[1])
    leaving.start()
    leaving.wait()


def pack_extra(plan, amps, extra, stage, sem):
    pack(plan, amps, [(extra, jnp.int32(0), jnp.int32(extra.shape[0]))], stage, sem)


def pack_rest(cap, live, row_tiles, chunks, start, where, plan, labels, amps, *rest):
    bufs = rest[: len(chunks)]
    table, listed, stage, sem, found, counts = rest[len(chunks) :]
    targets = []
    for buf, size in zip(bufs, chunks):
        targets.append((buf, jnp.int32(start), jnp.int32(start + size)))
        start = start + size
    pack(plan, amps, targets, stage, sem)
    list_tiles(cap, live, row_tiles, where[1], labels, table, listed, found, counts)


def extra_sizes(most):
    return [size for size in SIZES if size < most] + [most]


def rest_of(most, chunks, sizes):
    over = most - sum(chunks)
    size = jnp.int32(sizes[0])
    for low, high in zip(sizes, sizes[1:]):
        size = jnp.where(over > low, high, size)
    return size


def place_kernel(part, whole, held, sem):
    coming = pltpu.make_async_copy(part, held, sem.at[0])
    coming.start()
    coming.wait()
    leaving = pltpu.make_async_copy(held, whole.at[pl.ds(0, held.shape[0])], sem.at[1])
    leaving.start()
    leaving.wait()


def placed(part, size):
    any_space = pl.BlockSpec(memory_space=pl.ANY)
    return pl.pallas_call(
        place_kernel,
        out_shape=jax.ShapeDtypeStruct((size,) + part.shape[1:], part.dtype),
        in_specs=[any_space],
        out_specs=any_space,
        scratch_shapes=[pltpu.VMEM(part.shape, part.dtype), pltpu.SemaphoreType.DMA((2,))],
        compiler_params=pltpu.CompilerParams(vmem_limit_bytes=16 * 1024 * 1024),
        name="placed",
    )(part)


def depth_for(pairs):
    depths = [depth for depth in DEPTHS if depth < NT // 2] + [NT // 2]
    wanted = jnp.int32(depths[0])
    for low, high in zip(depths, depths[1:]):
        wanted = jnp.where(pairs > low, high, wanted)
    return wanted, depths


def list_tiles(cap, live, row_tiles, blk, labels, table, listed, found, counts):
    blocks = row_tiles // PAIR

    def clear(block, carry):
        counts[block] = 0
        for column in range(NT):
            found[block, column] = -1
            table[block, column] = 0
        return carry

    lax.fori_loop(0, blocks, clear, 0)

    def of_owner(owner, count):
        for position in range(cap):
            label = labels[owner, live + position]

            @pl.when(label >= 0)
            def _(count=count):
                place = by24(label)
                column = label - place * NT - blk * row_tiles
                column = jnp.where(column < 0, column + NT, column)
                block = lax.shift_right_logical(place, 1)
                held = found[block, column]
                known = counts[block]
                at = jnp.where(held < 0, known, held)
                found[block, column] = at
                counts[block] = jnp.where(held < 0, known + 1, known)
                table[block, at] = column
                listed[0, count] = owner * cap + position
                listed[1, count] = place
                listed[2, count] = at

            count = count + (label >= 0).astype(jnp.int32)
        return count

    total = lax.fori_loop(0, labels.shape[0], of_owner, jnp.int32(0))
    pairs = lax.fori_loop(
        0, blocks, lambda block, most: jnp.maximum(most, (counts[block] + 1) // 2), jnp.int32(1)
    )
    table[blocks, 0] = pairs
    listed[3, 0] = total


def build_w(table, listed, tiles, w_out, w, sem):
    wanted, _ = depth_for(table[table.shape[0] - 1, 0])
    total = listed[3, 0]

    def zero(pair, carry):
        at = pl.ds(pl.multiple_of(pair * 2 * TILE, 2 * TILE), 2 * TILE)
        w[:, at] = jnp.zeros((w.shape[0], 2 * TILE), w.dtype)
        return carry

    lax.fori_loop(0, wanted, zero, 0)

    def tile_in(index):
        rows = pl.ds(pl.multiple_of(listed[1, index] * TILE, TILE), TILE)
        at = pl.ds(pl.multiple_of(listed[2, index] * TILE, TILE), TILE)
        return pltpu.make_async_copy(tiles.at[listed[0, index]], w.at[rows, at], sem.at[0])

    def start_in(index, carry):
        tile_in(index).start()
        return carry

    def landed(index, carry):
        tile_in(0).wait()
        return carry

    lax.fori_loop(0, total, start_in, 0)
    lax.fori_loop(0, total, landed, 0)

    def pair_out(pair):
        at = pl.ds(pl.multiple_of(pair * 2 * TILE, 2 * TILE), 2 * TILE)
        return pltpu.make_async_copy(w.at[:, at], w_out.at[:, at], sem.at[1])

    def start_out(pair, carry):
        pair_out(pair).start()
        return carry

    def left(pair, carry):
        pair_out(pair).wait()
        return carry

    lax.fori_loop(0, wanted, start_out, 0)
    lax.fori_loop(0, wanted, left, 0)


def cycle_kernel(
    row_tiles, early, chunks, sizes, stage, plan, table, energy, eps_row, eps_col, w_in,
    amps, bare, early_buf, prev_buf, this_buf, out_in, out, w, x, held, made, sems, w_sem,
):
    del out_in
    half = row_tiles * TILE
    pairs = table[row_tiles // PAIR, 0]
    steps = NT // STEP
    cols = STEP * TILE
    shift = rest_of(plan[11, 0], chunks, sizes)
    total = plan[6, 0]

    def slot_at(column):
        return jnp.where(column >= NT, total, plan[5, jnp.minimum(column, NT - 1)])

    def complete(limit):
        def one(step, count):
            return count + (slot_at((step + 1) * STEP) <= limit).astype(jnp.int32)

        return lax.fori_loop(0, steps, one, jnp.int32(0))

    ends = [jnp.int32(0)] + [shift + sum(chunks[:index]) for index in range(len(chunks) + 1)]
    begin = jnp.int32(0) if stage == 0 else complete(ends[stage])
    end = jnp.int32(steps) if stage == len(chunks) else complete(ends[stage + 1])
    split = ends[stage]
    prev_start = 0 if stage == 0 else ends[stage - 1]

    def dense_copies(step, slot):
        at = pl.ds(pl.multiple_of(step * cols, cols), cols)
        return (
            pltpu.make_async_copy(amps.at[0, :, at], x.at[slot, :half], sems.at[0, slot]),
            pltpu.make_async_copy(bare.at[0, :, at], held.at[slot], sems.at[1, slot]),
        )

    def out_copy(step, slot):
        at = pl.ds(pl.multiple_of(step * cols, cols), cols)
        return pltpu.make_async_copy(made.at[slot], out.at[0, :, at], sems.at[3, slot])

    def tile_copy(source, place, at, slot):
        rows = pl.ds(pl.multiple_of(half + place * TILE, TILE), TILE)
        return pltpu.make_async_copy(source, x.at[slot, rows, at * TILE : (at + 1) * TILE], sems.at[2, slot])

    def early_at(column):
        known = jnp.where(column >= NT, plan[12, 0], plan[10, jnp.minimum(column, NT - 1)])
        return jnp.minimum(known, early)

    def issue(step, slot):
        for copy in dense_copies(step, slot):
            copy.start()
        for at in range(STEP):
            column = step * STEP + at
            lanes = slice(at * TILE, (at + 1) * TILE)
            x[slot, half:, lanes] = jnp.zeros((half, TILE), x.dtype)
            low, high = slot_at(column), slot_at(column + 1)
            middle = jnp.clip(split, low, high)

            def from_buf(buf, base, line, at=at):
                def one(index, carry):
                    tile_copy(buf.at[index - base], plan[line, index], at, slot).start()
                    return carry

                return one

            lax.fori_loop(early_at(column), early_at(column + 1), from_buf(early_buf, 0, 8), 0)
            lax.fori_loop(low, middle, from_buf(prev_buf, prev_start, 3), 0)
            lax.fori_loop(middle, high, from_buf(this_buf, split, 3), 0)

    def masked(base, line, column, at, slot):
        for place in range(row_tiles):

            @pl.when(plan[line, place * NT + column] == 0)
            def _():
                rows = slice(base + place * TILE, base + (place + 1) * TILE)
                x[slot, rows, at * TILE : (at + 1) * TILE] = jnp.zeros((TILE, TILE), x.dtype)

    def arrive(step, slot):
        for copy in dense_copies(step, slot):
            copy.wait()
        for at in range(STEP):
            masked(0, 7, step * STEP + at, at, slot)

        def landed(index, carry):
            tile_copy(this_buf.at[0], 0, 0, slot).wait()
            return carry

        first, last = step * STEP, (step + 1) * STEP
        lax.fori_loop(0, early_at(last) - early_at(first) + slot_at(last) - slot_at(first), landed, 0)

    def product(step, slot, depth):
        at = pl.ds(pl.multiple_of(step * cols, cols), cols)
        for block in range(row_tiles // PAIR):
            rows = slice(block * PAIR * TILE, (block + 1) * PAIR * TILE)
            acc = None
            for pair in range(depth):
                pieces = []
                for index in (2 * pair, 2 * pair + 1):
                    place = pl.multiple_of(table[block, index] * TILE, TILE)
                    pieces.append(x[slot, pl.ds(place, TILE), :])
                part = jnp.dot(
                    w[rows, pair * 2 * TILE : (pair + 1) * 2 * TILE],
                    jnp.concatenate(pieces, axis=0),
                    preferred_element_type=jnp.float32,
                )
                acc = part if acc is None else acc + part
            denom = eps_row[rows, :] + eps_col[:, at] - energy[0]
            value = (held[slot, rows, :].astype(jnp.float32) + acc) / denom
            for part in range(PAIR):
                place = block * PAIR + part
                for column in range(STEP):
                    kept = plan[7, place * NT + step * STEP + column].astype(jnp.float32)
                    lanes = slice(column * TILE, (column + 1) * TILE)
                    piece = value[part * TILE : (part + 1) * TILE, lanes] * kept
                    made[slot, place * TILE : (place + 1) * TILE, lanes] = piece.astype(made.dtype)

    def w_copy(pair):
        at = pl.ds(pl.multiple_of(pair * 2 * TILE, 2 * TILE), 2 * TILE)
        return pltpu.make_async_copy(w_in.at[:, at], w.at[:, at], w_sem)

    @pl.when(begin < end)
    def _():
        wanted, depths = depth_for(pairs)

        def load(pair, carry):
            w_copy(pair).start()
            return carry

        lax.fori_loop(0, wanted, load, 0)
        issue(begin, lax.rem(begin, 2))

        def loaded(pair, carry):
            w_copy(pair).wait()
            return carry

        lax.fori_loop(0, wanted, loaded, 0)

        def one(step, carry):
            slot = lax.rem(step, 2)

            @pl.when(step + 1 < end)
            def _():
                issue(step + 1, 1 - slot)

            arrive(step, slot)

            @pl.when(step >= begin + 2)
            def _():
                out_copy(step - 2, slot).wait()

            for depth in depths:
                pl.when(wanted == depth)(functools.partial(product, step, slot, depth))
            out_copy(step, slot).start()
            return carry

        lax.fori_loop(begin, end, one, 0)

        @pl.when(end >= begin + 2)
        def _():
            out_copy(end - 2, lax.rem(end, 2)).wait()

        out_copy(end - 1, lax.rem(end - 1, 2)).wait()


def screened_exchange(amplitudes, amp_mask, bare_ints, int_tiles, tile_ids, eps_virt, eps_pair):
    pairs, panel_rows, width = amplitudes.shape
    row_tiles = panel_rows // TILE
    cap = tile_ids.shape[2]
    owners = lax.axis_size("own")
    own, blk = lax.axis_index("own"), lax.axis_index("blk")
    where = jnp.stack([own, blk]).astype(jnp.int32)
    early, chunks = EARLY, CHUNKS
    most_extra = row_tiles * NT - sum(chunks)
    sizes = extra_sizes(most_extra)
    any_space = pl.BlockSpec(memory_space=pl.ANY)
    in_hbm = pl.BlockSpec(memory_space=pltpu.HBM)
    smem = pl.BlockSpec(memory_space=pltpu.SMEM)
    vmem = pl.BlockSpec(memory_space=pltpu.VMEM)

    tiles = lax.all_gather(int_tiles, "own", axis=1, tiled=True).reshape(-1, TILE, TILE)

    live = row_tiles * NT
    wide = -(-(live + cap) // TILE) * TILE
    told = jnp.concatenate([amp_mask.reshape(1, -1), tile_ids.reshape(1, -1)], axis=1)
    told = jnp.pad(told, ((0, 0), (0, wide - live - cap)), constant_values=-1)
    partner_told = passed_along(told, "blk", 1)
    tile_type = lambda count: jax.ShapeDtypeStruct((count, TILE, TILE), amplitudes.dtype)
    params = pltpu.CompilerParams(vmem_limit_bytes=VMEM)
    light = pl.CostEstimate(flops=1, bytes_accessed=1, transcendentals=0)
    early_tiles = pl.pallas_call(
        functools.partial(pack_early, row_tiles),
        out_shape=tile_type(early),
        in_specs=[smem, in_hbm],
        out_specs=in_hbm,
        scratch_shapes=[pltpu.VMEM((early, TILE, TILE), amplitudes.dtype), pltpu.SemaphoreType.DMA((2,))],
        compiler_params=params,
        cost_estimate=light,
        name="pack_early",
    )(amp_mask, amplitudes)
    partner_told, early_tiles = lax.optimization_barrier((partner_told, early_tiles))
    early_buf = passed_along(early_tiles, "blk", 1)
    told = jnp.broadcast_to(jnp.concatenate([told, partner_told], axis=1), (owners, 2 * wide))
    info = lax.all_to_all(told, "own", 0, 0, tiled=True)

    plan = pl.pallas_call(
        functools.partial(make_plan, row_tiles, cap, early),
        out_shape=jax.ShapeDtypeStruct((16, wide), jnp.int32),
        in_specs=[smem, vmem],
        out_specs=vmem,
        compiler_params=params,
        cost_estimate=light,
        name="make_plan",
    )(where, info)
    blocks = row_tiles // PAIR
    labels = info[:, :wide]

    def branch(size):
        def send(where, plan, labels, amplitudes):
            extra = pl.pallas_call(
                pack_extra,
                out_shape=tile_type(size),
                in_specs=[smem, in_hbm],
                out_specs=in_hbm,
                scratch_shapes=[
                    pltpu.VMEM((size, TILE, TILE), amplitudes.dtype),
                    pltpu.SemaphoreType.DMA((2,)),
                ],
                compiler_params=params,
                cost_estimate=light,
                name="pack_extra",
            )(plan, amplitudes)
            moved = passed_along(extra, "blk", 1)
            *others, table, listed = pl.pallas_call(
                functools.partial(pack_rest, cap, live, row_tiles, chunks, size),
                out_shape=[tile_type(count) for count in chunks]
                + [
                    jax.ShapeDtypeStruct((blocks + 1, NT), jnp.int32),
                    jax.ShapeDtypeStruct((4, owners * cap), jnp.int32),
                ],
                in_specs=[smem, smem, smem, in_hbm],
                out_specs=[in_hbm] * len(chunks) + [smem, smem],
                scratch_shapes=[
                    pltpu.VMEM((sum(chunks), TILE, TILE), amplitudes.dtype),
                    pltpu.SemaphoreType.DMA((2,)),
                    pltpu.SMEM((blocks, NT), jnp.int32),
                    pltpu.SMEM((blocks,), jnp.int32),
                ],
                compiler_params=params,
                cost_estimate=light,
                name="pack_rest",
            )(where, plan, labels, amplitudes)
            return (placed(moved, sizes[-1]), table, listed, *others)

        return send

    place = sum((plan[11, 0] - sum(chunks) > size).astype(jnp.int32) for size in sizes[:-1])
    got, table, listed, *others = lax.switch(
        place, [branch(size) for size in sizes], where, plan, labels, amplitudes
    )
    got, first = lax.optimization_barrier((got, others[0]))
    bufs = [got, passed_along(first, "blk", 1)]
    w = pl.pallas_call(
        build_w,
        out_shape=jax.ShapeDtypeStruct((panel_rows, width), jnp.bfloat16),
        in_specs=[smem, smem, any_space],
        out_specs=in_hbm,
        scratch_shapes=[pltpu.VMEM((panel_rows, width), jnp.bfloat16), pltpu.SemaphoreType.DMA((2,))],
        compiler_params=params,
        name="build_w",
    )(table, listed, tiles)
    w, second = lax.optimization_barrier((w, others[1]))
    bufs.append(passed_along(second, "blk", 1))
    eps_row = lax.dynamic_slice_in_dim(eps_virt, blk * panel_rows, panel_rows, 0).reshape(panel_rows, 1)
    eps_col = eps_virt.reshape(1, width)
    cols = STEP * TILE
    out = None
    for stage in range(len(chunks) + 1):
        prev_buf = bufs[max(stage - 1, 0)]
        operands = [
            plan, table, eps_pair, eps_row, eps_col, w, amplitudes, bare_ints, early_buf,
            prev_buf, bufs[stage], bare_ints if out is None else out,
        ]
        out = pl.pallas_call(
            functools.partial(cycle_kernel, row_tiles, early, chunks, sizes, stage),
            out_shape=jax.ShapeDtypeStruct(amplitudes.shape, amplitudes.dtype),
            in_specs=[smem] * 3 + [vmem] * 2 + [any_space] + [in_hbm] * 2 + [any_space] * 3 + [in_hbm],
            out_specs=in_hbm,
            input_output_aliases={} if out is None else {11: 0},
            scratch_shapes=[
                pltpu.VMEM((panel_rows, width), jnp.bfloat16),
                pltpu.VMEM((2, width, cols), jnp.bfloat16),
                pltpu.VMEM((2, panel_rows, cols), jnp.bfloat16),
                pltpu.VMEM((2, panel_rows, cols), jnp.bfloat16),
                pltpu.SemaphoreType.DMA((4, 2)),
                pltpu.SemaphoreType.DMA,
            ],
            compiler_params=params,
            cost_estimate=pl.CostEstimate(
                flops=2 * panel_rows * width * width // len(chunks),
                bytes_accessed=4 * panel_rows * width * 2 // len(chunks),
                transcendentals=0,
            ),
            name=f"cycle_{stage}",
        )(*operands)
        if len(bufs) < len(chunks) + 1:
            out, following = lax.optimization_barrier((out, others[len(bufs) - 1]))
            bufs.append(passed_along(following, "blk", 1))
    return out


def ring_exchange(amplitudes, amp_mask, bare_ints, int_tiles, tile_ids, eps_virt, eps_pair):
    pairs, panel_rows, width = amplitudes.shape
    row_tiles = panel_rows // TILE
    slots = row_tiles * NT
    mask_cells = jnp.broadcast_to(
        amp_mask.astype(jnp.bfloat16)[:, :, None, :, None], (pairs, row_tiles, TILE, NT, TILE)
    ).reshape(pairs, panel_rows, width)
    screened = amplitudes * mask_cells
    tiles = lax.all_gather(int_tiles, "own", axis=1, tiled=True)
    labels = lax.all_gather(tile_ids, "own", axis=1, tiled=True)
    flat_labels = labels.reshape(-1)
    flat_tiles = tiles.reshape(-1, TILE, TILE)
    onehot = (flat_labels[:, None] == jnp.arange(slots, dtype=jnp.int32)[None, :]).astype(jnp.bfloat16)
    grid = jnp.einsum("sq,sij->qij", onehot, flat_tiles, preferred_element_type=jnp.float32)
    w_rows = (
        grid.astype(jnp.bfloat16)
        .reshape(row_tiles, NT, TILE, TILE)
        .transpose(0, 2, 1, 3)
        .reshape(panel_rows, width)
    )
    position = lax.axis_index("blk")
    stops = lax.axis_size("blk")
    panel = screened
    cycle_sum = jnp.zeros((pairs, panel_rows, width), jnp.float32)
    for stop in range(stops):
        columns = lax.dynamic_slice_in_dim(w_rows, (position - stop) % stops * panel_rows, panel_rows, 1)
        cycle_sum = cycle_sum + jnp.einsum("ac,pcb->pab", columns, panel, preferred_element_type=jnp.float32)
        if stop + 1 < stops:
            panel = passed_along(panel, "blk", 1)
    rows_energy = lax.dynamic_slice_in_dim(eps_virt, position * panel_rows, panel_rows, 0)
    denom = rows_energy[None, :, None] + eps_virt[None, None, :] - eps_pair[:, None, None]
    updated = (bare_ints.astype(jnp.float32) + cycle_sum) / denom * mask_cells.astype(jnp.float32)
    return updated.astype(jnp.bfloat16)


def solution(mesh):
    local = screened_exchange if mesh.shape["blk"] == 2 else ring_exchange
    in_specs = (
        P("own", "blk", None),
        P("own", "blk", None),
        P("own", "blk", None),
        P("blk", "own", None, None, None),
        P("blk", "own", None),
        P(),
        P("own"),
    )
    out_specs = P("own", "blk", None)
    return jax.shard_map(local, mesh=mesh, in_specs=in_specs, out_specs=out_specs, check_vma=False)
```

```python
import functools

import jax
import jax.numpy as jnp
from jax import lax
from jax.experimental import pallas as pl
from jax.experimental.pallas import tpu as pltpu
from jax.sharding import PartitionSpec as P

TILE = 128
NT = 24
STEP = 2
EARLY = 28
CHUNKS = (48, 40, 16)
SIZES = (16, 24, 32, 40, 48, 64)
PAIR = 2
DEPTHS = (4, 6)
GROUP = 8
VMEM = 55 * 1024 * 1024


def passed_along(value, axis, steps):
    count = lax.axis_size(axis)
    pairs = [(source, (source + steps) % count) for source in range(count)]
    return lax.ppermute(value, axis, pairs)


def by24(index):
    return (index * 2731) >> 16


def make_plan(row_tiles, cap, early, where, info, plan_out):
    width = info.shape[1] // 2
    live = row_tiles * NT
    own, blk = where[0], where[1]
    infos = [info[:, :width], info[:, width:]]
    row = lax.broadcasted_iota(jnp.int32, (width, width), 0)
    lane = lax.broadcasted_iota(jnp.int32, (width, width), 1)
    row_hi, lane_hi = by24(row), by24(lane)
    row_lo, lane_lo = row - row_hi * NT, lane - lane_hi * NT
    same_lo = (row_lo == lane_lo).astype(jnp.float32)
    row_key, lane_key = row_lo * row_tiles + row_hi, lane_lo * row_tiles + lane_hi
    ahead = ((row_key < lane_key) & (row < live)).astype(jnp.bfloat16)
    places = lax.broadcasted_iota(jnp.int32, (8, width), 1)
    places_hi = by24(places)
    which = lax.broadcasted_iota(jnp.int32, (8, width), 0)
    digits = jnp.where(which == 0, places_hi, jnp.where(which == 1, places - places_hi * NT, 0))
    digits = digits.astype(jnp.bfloat16)
    owners = info.shape[0]
    mine = (lax.broadcasted_iota(jnp.int32, (owners, 1), 0) == own).astype(jnp.float32)
    lanes = lax.broadcasted_iota(jnp.int32, (owners, width), 1)

    def before(flags):
        return jnp.dot(flags.astype(jnp.bfloat16), ahead, preferred_element_type=jnp.float32)

    def listed(flags, count_before):
        count_column = jnp.sum(jnp.where(row == lane, count_before, 0.0), axis=1, keepdims=True)
        flag_column = jnp.sum(jnp.where(row == lane, flags, 0.0), axis=1, keepdims=True)
        onehot = jnp.where(count_column == lane.astype(jnp.float32), flag_column, 0.0)
        return jnp.dot(digits, onehot.astype(jnp.bfloat16), preferred_element_type=jnp.float32)

    masks = [
        jnp.broadcast_to(
            jnp.sum(jnp.where(lanes < live, info, 0).astype(jnp.float32) * mine, axis=0, keepdims=True), (8, width)
        )
        for info in infos
    ]

    most = jnp.int32(0)
    found = []
    for g in range(2):
        h = 1 - g
        seen = jnp.zeros((owners, width), jnp.float32)
        for slot in range(cap):
            seen = seen + (infos[g][:, live + slot : live + slot + 1] == lanes).astype(jnp.float32)
        seen = jnp.sum(seen, axis=0, keepdims=True)
        left = jnp.where(row_hi == lane_hi, seen, 0.0).astype(jnp.bfloat16)
        sender = 1 - blk if g == 0 else blk
        right = (row_lo == sender * row_tiles + lane_hi).astype(jnp.bfloat16)
        meets = jnp.dot(left, right, preferred_element_type=jnp.float32) * same_lo
        hits = jnp.dot(masks[g].astype(jnp.bfloat16), meets.astype(jnp.bfloat16), preferred_element_type=jnp.float32)
        need = jnp.where(hits > 0.5, masks[h], 0.0)
        kept_before = before(masks[h])
        late = jnp.where(kept_before >= early, need, 0.0)
        count = jnp.sum(late, axis=1, keepdims=True)
        most = jnp.maximum(most, jnp.max(count).astype(jnp.int32))
        found.append((late, before(late), count, kept_before))

    def write(lines):
        for index, line in lines.items():
            plan_out[index : index + 1, :] = jnp.broadcast_to(line[:1].astype(jnp.int32), (1, width))

    late, late_before, count, _ = found[1]
    sent_list = listed(late[:1], late_before[:1])
    write({0: sent_list[0:1], 1: sent_list[1:2], 2: count, 7: masks[0]})
    plan_out[11:12, :] = jnp.broadcast_to(most, (1, width))
    late, late_before, count, kept_before = found[0]
    late_list = listed(late[:1], late_before[:1])
    early_list = listed(masks[1][:1], kept_before[:1])
    total = jnp.sum(masks[1], axis=1, keepdims=True)
    write({3: late_list[0:1], 4: late_list[1:2], 5: late_before, 6: count})
    write({8: early_list[0:1], 9: early_list[1:2], 10: kept_before, 12: total})


def pack(plan, amps, targets, stage, sem):
    total = plan[2, 0]

    def tile_in(slot, place):
        row = pl.ds(pl.multiple_of(plan[0, slot] * TILE, TILE), TILE)
        column = pl.ds(pl.multiple_of(plan[1, slot] * TILE, TILE), TILE)
        return pltpu.make_async_copy(amps.at[0, row, column], stage.at[place], sem.at[0])

    def group_out(buf, group, place):
        return pltpu.make_async_copy(
            stage.at[pl.ds(place + group * GROUP, GROUP)], buf.at[pl.ds(group * GROUP, GROUP)], sem.at[1]
        )

    places = []
    place = 0
    for buf, start, stop in targets:
        end = jnp.clip(total, start, stop)

        def one(slot, carry, place=place, start=start):
            tile_in(slot, place + slot - start).start()
            return carry

        lax.fori_loop(start, end, one, 0)
        places.append((buf, place, end - start))
        place = place + buf.shape[0]
    for _, _, count in places:

        def landed(slot, carry):
            tile_in(0, 0).wait()
            return carry

        lax.fori_loop(0, count, landed, 0)
    groups = [(buf, place, (count + GROUP - 1) // GROUP) for buf, place, count in places]
    for buf, place, count in groups:

        def store(group, carry, buf=buf, place=place):
            group_out(buf, group, place).start()
            return carry

        lax.fori_loop(0, count, store, 0)
    for buf, place, count in groups:

        def stored(group, carry, buf=buf):
            group_out(buf, 0, 0).wait()
            return carry

        lax.fori_loop(0, count, stored, 0)


def pack_early(row_tiles, mask, amps, buf, stage, sem):
    count = buf.shape[0]

    def tile_in(place, column, at):
        rows = pl.ds(pl.multiple_of(place * TILE, TILE), TILE)
        lanes = pl.ds(pl.multiple_of(column * TILE, TILE), TILE)
        return pltpu.make_async_copy(amps.at[0, rows, lanes], stage.at[at], sem.at[0])

    def one_column(state):
        column, found = state
        for place in range(row_tiles):
            kept = (mask[0, place, column] > 0) & (found < count)
            pl.when(kept)(lambda place=place, found=found: tile_in(place, column, found).start())
            found = found + kept.astype(jnp.int32)
        return column + 1, found

    _, found = lax.while_loop(
        lambda state: (state[0] < NT) & (state[1] < count), one_column, (jnp.int32(0), jnp.int32(0))
    )

    def landed(index, carry):
        tile_in(0, 0, 0).wait()
        return carry

    lax.fori_loop(0, found, landed, 0)
    leaving = pltpu.make_async_copy(stage, buf, sem.at[1])
    leaving.start()
    leaving.wait()


def pack_extra(plan, amps, extra, stage, sem):
    pack(plan, amps, [(extra, jnp.int32(0), jnp.int32(extra.shape[0]))], stage, sem)


def pack_rest(cap, live, row_tiles, chunks, start, where, plan, labels, amps, *rest):
    bufs = rest[: len(chunks)]
    table, listed, stage, sem, found, counts = rest[len(chunks) :]
    targets = []
    for buf, size in zip(bufs, chunks):
        targets.append((buf, jnp.int32(start), jnp.int32(start + size)))
        start = start + size
    pack(plan, amps, targets, stage, sem)
    list_tiles(cap, live, row_tiles, where[1], labels, table, listed, found, counts)


def extra_sizes(most):
    return [size for size in SIZES if size < most] + [most]


def rest_of(most, chunks, sizes):
    over = most - sum(chunks)
    size = jnp.int32(sizes[0])
    for low, high in zip(sizes, sizes[1:]):
        size = jnp.where(over > low, high, size)
    return size


def place_kernel(part, whole, held, sem):
    coming = pltpu.make_async_copy(part, held, sem.at[0])
    coming.start()
    coming.wait()
    leaving = pltpu.make_async_copy(held, whole.at[pl.ds(0, held.shape[0])], sem.at[1])
    leaving.start()
    leaving.wait()


def placed(part, size):
    any_space = pl.BlockSpec(memory_space=pl.ANY)
    return pl.pallas_call(
        place_kernel,
        out_shape=jax.ShapeDtypeStruct((size,) + part.shape[1:], part.dtype),
        in_specs=[any_space],
        out_specs=any_space,
        scratch_shapes=[pltpu.VMEM(part.shape, part.dtype), pltpu.SemaphoreType.DMA((2,))],
        compiler_params=pltpu.CompilerParams(vmem_limit_bytes=16 * 1024 * 1024),
        name="placed",
    )(part)


def depth_for(pairs):
    depths = [depth for depth in DEPTHS if depth < NT // 2] + [NT // 2]
    wanted = jnp.int32(depths[0])
    for low, high in zip(depths, depths[1:]):
        wanted = jnp.where(pairs > low, high, wanted)
    return wanted, depths


def list_tiles(cap, live, row_tiles, blk, labels, table, listed, found, counts):
    blocks = row_tiles // PAIR

    def clear(block, carry):
        counts[block] = 0
        for column in range(NT):
            found[block, column] = -1
            table[block, column] = 0
        return carry

    lax.fori_loop(0, blocks, clear, 0)

    def of_owner(owner, count):
        for position in range(cap):
            label = labels[owner, live + position]

            @pl.when(label >= 0)
            def _(count=count):
                place = by24(label)
                column = label - place * NT - blk * row_tiles
                column = jnp.where(column < 0, column + NT, column)
                block = lax.shift_right_logical(place, 1)
                held = found[block, column]
                known = counts[block]
                at = jnp.where(held < 0, known, held)
                found[block, column] = at
                counts[block] = jnp.where(held < 0, known + 1, known)
                table[block, at] = column
                listed[0, count] = owner * cap + position
                listed[1, count] = place
                listed[2, count] = at

            count = count + (label >= 0).astype(jnp.int32)
        return count

    total = lax.fori_loop(0, labels.shape[0], of_owner, jnp.int32(0))
    pairs = lax.fori_loop(
        0, blocks, lambda block, most: jnp.maximum(most, (counts[block] + 1) // 2), jnp.int32(1)
    )
    table[blocks, 0] = pairs
    listed[3, 0] = total


def build_w(table, listed, tiles, w_out, w, sem):
    wanted, _ = depth_for(table[table.shape[0] - 1, 0])
    total = listed[3, 0]

    def zero(pair, carry):
        at = pl.ds(pl.multiple_of(pair * 2 * TILE, 2 * TILE), 2 * TILE)
        w[:, at] = jnp.zeros((w.shape[0], 2 * TILE), w.dtype)
        return carry

    lax.fori_loop(0, wanted, zero, 0)

    def tile_in(index):
        rows = pl.ds(pl.multiple_of(listed[1, index] * TILE, TILE), TILE)
        at = pl.ds(pl.multiple_of(listed[2, index] * TILE, TILE), TILE)
        return pltpu.make_async_copy(tiles.at[listed[0, index]], w.at[rows, at], sem.at[0])

    def start_in(index, carry):
        tile_in(index).start()
        return carry

    def landed(index, carry):
        tile_in(0).wait()
        return carry

    lax.fori_loop(0, total, start_in, 0)
    lax.fori_loop(0, total, landed, 0)

    def pair_out(pair):
        at = pl.ds(pl.multiple_of(pair * 2 * TILE, 2 * TILE), 2 * TILE)
        return pltpu.make_async_copy(w.at[:, at], w_out.at[:, at], sem.at[1])

    def start_out(pair, carry):
        pair_out(pair).start()
        return carry

    def left(pair, carry):
        pair_out(pair).wait()
        return carry

    lax.fori_loop(0, wanted, start_out, 0)
    lax.fori_loop(0, wanted, left, 0)


def cycle_kernel(
    row_tiles, early, chunks, sizes, stage, plan, table, energy, eps_row, eps_col, w_in,
    amps, bare, early_buf, prev_buf, this_buf, out_in, out, w, x, held, made, sems, w_sem,
):
    del out_in
    half = row_tiles * TILE
    pairs = table[row_tiles // PAIR, 0]
    steps = NT // STEP
    cols = STEP * TILE
    shift = rest_of(plan[11, 0], chunks, sizes)
    total = plan[6, 0]

    def slot_at(column):
        return jnp.where(column >= NT, total, plan[5, jnp.minimum(column, NT - 1)])

    def complete(limit):
        def one(step, count):
            return count + (slot_at((step + 1) * STEP) <= limit).astype(jnp.int32)

        return lax.fori_loop(0, steps, one, jnp.int32(0))

    ends = [jnp.int32(0)] + [shift + sum(chunks[:index]) for index in range(len(chunks) + 1)]
    begin = jnp.int32(0) if stage == 0 else complete(ends[stage])
    end = jnp.int32(steps) if stage == len(chunks) else complete(ends[stage + 1])
    split = ends[stage]
    prev_start = 0 if stage == 0 else ends[stage - 1]

    def dense_copies(step, slot):
        at = pl.ds(pl.multiple_of(step * cols, cols), cols)
        return (
            pltpu.make_async_copy(amps.at[0, :, at], x.at[slot, :half], sems.at[0, slot]),
            pltpu.make_async_copy(bare.at[0, :, at], held.at[slot], sems.at[1, slot]),
        )

    def out_copy(step, slot):
        at = pl.ds(pl.multiple_of(step * cols, cols), cols)
        return pltpu.make_async_copy(made.at[slot], out.at[0, :, at], sems.at[3, slot])

    def tile_copy(source, place, at, slot):
        rows = pl.ds(pl.multiple_of(half + place * TILE, TILE), TILE)
        return pltpu.make_async_copy(source, x.at[slot, rows, at * TILE : (at + 1) * TILE], sems.at[2, slot])

    def early_at(column):
        known = jnp.where(column >= NT, plan[12, 0], plan[10, jnp.minimum(column, NT - 1)])
        return jnp.minimum(known, early)

    def issue(step, slot):
        for copy in dense_copies(step, slot):
            copy.start()
        for at in range(STEP):
            column = step * STEP + at
            lanes = slice(at * TILE, (at + 1) * TILE)
            x[slot, half:, lanes] = jnp.zeros((half, TILE), x.dtype)
            low, high = slot_at(column), slot_at(column + 1)
            middle = jnp.clip(split, low, high)

            def from_buf(buf, base, line, at=at):
                def one(index, carry):
                    tile_copy(buf.at[index - base], plan[line, index], at, slot).start()
                    return carry

                return one

            lax.fori_loop(early_at(column), early_at(column + 1), from_buf(early_buf, 0, 8), 0)
            lax.fori_loop(low, middle, from_buf(prev_buf, prev_start, 3), 0)
            lax.fori_loop(middle, high, from_buf(this_buf, split, 3), 0)

    def masked(base, line, column, at, slot):
        for place in range(row_tiles):

            @pl.when(plan[line, place * NT + column] == 0)
            def _():
                rows = slice(base + place * TILE, base + (place + 1) * TILE)
                x[slot, rows, at * TILE : (at + 1) * TILE] = jnp.zeros((TILE, TILE), x.dtype)

    def arrive(step, slot):
        for copy in dense_copies(step, slot):
            copy.wait()
        for at in range(STEP):
            masked(0, 7, step * STEP + at, at, slot)

        def landed(index, carry):
            tile_copy(this_buf.at[0], 0, 0, slot).wait()
            return carry

        first, last = step * STEP, (step + 1) * STEP
        lax.fori_loop(0, early_at(last) - early_at(first) + slot_at(last) - slot_at(first), landed, 0)

    def product(step, slot, depth):
        at = pl.ds(pl.multiple_of(step * cols, cols), cols)
        for block in range(row_tiles // PAIR):
            rows = slice(block * PAIR * TILE, (block + 1) * PAIR * TILE)
            acc = None
            for pair in range(depth):
                pieces = []
                for index in (2 * pair, 2 * pair + 1):
                    place = pl.multiple_of(table[block, index] * TILE, TILE)
                    pieces.append(x[slot, pl.ds(place, TILE), :])
                part = jnp.dot(
                    w[rows, pair * 2 * TILE : (pair + 1) * 2 * TILE],
                    jnp.concatenate(pieces, axis=0),
                    preferred_element_type=jnp.float32,
                )
                acc = part if acc is None else acc + part
            denom = eps_row[rows, :] + eps_col[:, at] - energy[0]
            value = (held[slot, rows, :].astype(jnp.float32) + acc) / denom
            for part in range(PAIR):
                place = block * PAIR + part
                for column in range(STEP):
                    kept = plan[7, place * NT + step * STEP + column].astype(jnp.float32)
                    lanes = slice(column * TILE, (column + 1) * TILE)
                    piece = value[part * TILE : (part + 1) * TILE, lanes] * kept
                    made[slot, place * TILE : (place + 1) * TILE, lanes] = piece.astype(made.dtype)

    def w_copy(pair):
        at = pl.ds(pl.multiple_of(pair * 2 * TILE, 2 * TILE), 2 * TILE)
        return pltpu.make_async_copy(w_in.at[:, at], w.at[:, at], w_sem)

    @pl.when(begin < end)
    def _():
        wanted, depths = depth_for(pairs)

        def load(pair, carry):
            w_copy(pair).start()
            return carry

        lax.fori_loop(0, wanted, load, 0)
        issue(begin, lax.rem(begin, 2))

        def loaded(pair, carry):
            w_copy(pair).wait()
            return carry

        lax.fori_loop(0, wanted, loaded, 0)

        def one(step, carry):
            slot = lax.rem(step, 2)

            @pl.when(step + 1 < end)
            def _():
                issue(step + 1, 1 - slot)

            arrive(step, slot)

            @pl.when(step >= begin + 2)
            def _():
                out_copy(step - 2, slot).wait()

            for depth in depths:
                pl.when(wanted == depth)(functools.partial(product, step, slot, depth))
            out_copy(step, slot).start()
            return carry

        lax.fori_loop(begin, end, one, 0)

        @pl.when(end >= begin + 2)
        def _():
            out_copy(end - 2, lax.rem(end, 2)).wait()

        out_copy(end - 1, lax.rem(end - 1, 2)).wait()


def screened_exchange(amplitudes, amp_mask, bare_ints, int_tiles, tile_ids, eps_virt, eps_pair):
    pairs, panel_rows, width = amplitudes.shape
    row_tiles = panel_rows // TILE
    cap = tile_ids.shape[2]
    owners = lax.axis_size("own")
    own, blk = lax.axis_index("own"), lax.axis_index("blk")
    where = jnp.stack([own, blk]).astype(jnp.int32)
    early, chunks = EARLY, CHUNKS
    most_extra = row_tiles * NT - sum(chunks)
    sizes = extra_sizes(most_extra)
    any_space = pl.BlockSpec(memory_space=pl.ANY)
    in_hbm = pl.BlockSpec(memory_space=pltpu.HBM)
    smem = pl.BlockSpec(memory_space=pltpu.SMEM)
    vmem = pl.BlockSpec(memory_space=pltpu.VMEM)

    tiles = lax.all_gather(int_tiles, "own", axis=1, tiled=True).reshape(-1, TILE, TILE)

    live = row_tiles * NT
    wide = -(-(live + cap) // TILE) * TILE
    told = jnp.concatenate([amp_mask.reshape(1, -1), tile_ids.reshape(1, -1)], axis=1)
    told = jnp.pad(told, ((0, 0), (0, wide - live - cap)), constant_values=-1)
    partner_told = passed_along(told, "blk", 1)
    tile_type = lambda count: jax.ShapeDtypeStruct((count, TILE, TILE), amplitudes.dtype)
    params = pltpu.CompilerParams(vmem_limit_bytes=VMEM)
    light = pl.CostEstimate(flops=1, bytes_accessed=1, transcendentals=0)
    early_tiles = pl.pallas_call(
        functools.partial(pack_early, row_tiles),
        out_shape=tile_type(early),
        in_specs=[smem, in_hbm],
        out_specs=in_hbm,
        scratch_shapes=[pltpu.VMEM((early, TILE, TILE), amplitudes.dtype), pltpu.SemaphoreType.DMA((2,))],
        compiler_params=params,
        cost_estimate=light,
        name="pack_early",
    )(amp_mask, amplitudes)
    partner_told, early_tiles = lax.optimization_barrier((partner_told, early_tiles))
    early_buf = passed_along(early_tiles, "blk", 1)
    told = jnp.broadcast_to(jnp.concatenate([told, partner_told], axis=1), (owners, 2 * wide))
    info = lax.all_to_all(told, "own", 0, 0, tiled=True)

    plan = pl.pallas_call(
        functools.partial(make_plan, row_tiles, cap, early),
        out_shape=jax.ShapeDtypeStruct((16, wide), jnp.int32),
        in_specs=[smem, vmem],
        out_specs=vmem,
        compiler_params=params,
        cost_estimate=light,
        name="make_plan",
    )(where, info)
    blocks = row_tiles // PAIR
    labels = info[:, :wide]

    def branch(size):
        def send(where, plan, labels, amplitudes):
            extra = pl.pallas_call(
                pack_extra,
                out_shape=tile_type(size),
                in_specs=[smem, in_hbm],
                out_specs=in_hbm,
                scratch_shapes=[
                    pltpu.VMEM((size, TILE, TILE), amplitudes.dtype),
                    pltpu.SemaphoreType.DMA((2,)),
                ],
                compiler_params=params,
                cost_estimate=light,
                name="pack_extra",
            )(plan, amplitudes)
            moved = passed_along(extra, "blk", 1)
            *others, table, listed = pl.pallas_call(
                functools.partial(pack_rest, cap, live, row_tiles, chunks, size),
                out_shape=[tile_type(count) for count in chunks]
                + [
                    jax.ShapeDtypeStruct((blocks + 1, NT), jnp.int32),
                    jax.ShapeDtypeStruct((4, owners * cap), jnp.int32),
                ],
                in_specs=[smem, smem, smem, in_hbm],
                out_specs=[in_hbm] * len(chunks) + [smem, smem],
                scratch_shapes=[
                    pltpu.VMEM((sum(chunks), TILE, TILE), amplitudes.dtype),
                    pltpu.SemaphoreType.DMA((2,)),
                    pltpu.SMEM((blocks, NT), jnp.int32),
                    pltpu.SMEM((blocks,), jnp.int32),
                ],
                compiler_params=params,
                cost_estimate=light,
                name="pack_rest",
            )(where, plan, labels, amplitudes)
            return (placed(moved, sizes[-1]), table, listed, *others)

        return send

    place = sum((plan[11, 0] - sum(chunks) > size).astype(jnp.int32) for size in sizes[:-1])
    got, table, listed, *others = lax.switch(
        place, [branch(size) for size in sizes], where, plan, labels, amplitudes
    )
    got, first = lax.optimization_barrier((got, others[0]))
    bufs = [got, passed_along(first, "blk", 1)]
    w = pl.pallas_call(
        build_w,
        out_shape=jax.ShapeDtypeStruct((panel_rows, width), jnp.bfloat16),
        in_specs=[smem, smem, any_space],
        out_specs=in_hbm,
        scratch_shapes=[pltpu.VMEM((panel_rows, width), jnp.bfloat16), pltpu.SemaphoreType.DMA((2,))],
        compiler_params=params,
        name="build_w",
    )(table, listed, tiles)
    w, second = lax.optimization_barrier((w, others[1]))
    bufs.append(passed_along(second, "blk", 1))
    eps_row = lax.dynamic_slice_in_dim(eps_virt, blk * panel_rows, panel_rows, 0).reshape(panel_rows, 1)
    eps_col = eps_virt.reshape(1, width)
    cols = STEP * TILE
    out = None
    for stage in range(len(chunks) + 1):
        prev_buf = bufs[max(stage - 1, 0)]
        operands = [
            plan, table, eps_pair, eps_row, eps_col, w, amplitudes, bare_ints, early_buf,
            prev_buf, bufs[stage], bare_ints if out is None else out,
        ]
        out = pl.pallas_call(
            functools.partial(cycle_kernel, row_tiles, early, chunks, sizes, stage),
            out_shape=jax.ShapeDtypeStruct(amplitudes.shape, amplitudes.dtype),
            in_specs=[smem] * 3 + [vmem] * 2 + [any_space] + [in_hbm] * 2 + [any_space] * 3 + [in_hbm],
            out_specs=in_hbm,
            input_output_aliases={} if out is None else {11: 0},
            scratch_shapes=[
                pltpu.VMEM((panel_rows, width), jnp.bfloat16),
                pltpu.VMEM((2, width, cols), jnp.bfloat16),
                pltpu.VMEM((2, panel_rows, cols), jnp.bfloat16),
                pltpu.VMEM((2, panel_rows, cols), jnp.bfloat16),
                pltpu.SemaphoreType.DMA((4, 2)),
                pltpu.SemaphoreType.DMA,
            ],
            compiler_params=params,
            cost_estimate=pl.CostEstimate(
                flops=2 * panel_rows * width * width // len(chunks),
                bytes_accessed=4 * panel_rows * width * 2 // len(chunks),
                transcendentals=0,
            ),
            name=f"cycle_{stage}",
        )(*operands)
        if len(bufs) < len(chunks) + 1:
            out, following = lax.optimization_barrier((out, others[len(bufs) - 1]))
            bufs.append(passed_along(following, "blk", 1))
    return out


def ring_exchange(amplitudes, amp_mask, bare_ints, int_tiles, tile_ids, eps_virt, eps_pair):
    pairs, panel_rows, width = amplitudes.shape
    row_tiles = panel_rows // TILE
    slots = row_tiles * NT
    mask_cells = jnp.broadcast_to(
        amp_mask.astype(jnp.bfloat16)[:, :, None, :, None], (pairs, row_tiles, TILE, NT, TILE)
    ).reshape(pairs, panel_rows, width)
    screened = amplitudes * mask_cells
    tiles = lax.all_gather(int_tiles, "own", axis=1, tiled=True)
    labels = lax.all_gather(tile_ids, "own", axis=1, tiled=True)
    flat_labels = labels.reshape(-1)
    flat_tiles = tiles.reshape(-1, TILE, TILE)
    onehot = (flat_labels[:, None] == jnp.arange(slots, dtype=jnp.int32)[None, :]).astype(jnp.bfloat16)
    grid = jnp.einsum("sq,sij->qij", onehot, flat_tiles, preferred_element_type=jnp.float32)
    w_rows = (
        grid.astype(jnp.bfloat16)
        .reshape(row_tiles, NT, TILE, TILE)
        .transpose(0, 2, 1, 3)
        .reshape(panel_rows, width)
    )
    position = lax.axis_index("blk")
    stops = lax.axis_size("blk")
    panel = screened
    cycle_sum = jnp.zeros((pairs, panel_rows, width), jnp.float32)
    for stop in range(stops):
        columns = lax.dynamic_slice_in_dim(w_rows, (position - stop) % stops * panel_rows, panel_rows, 1)
        cycle_sum = cycle_sum + jnp.einsum("ac,pcb->pab", columns, panel, preferred_element_type=jnp.float32)
        if stop + 1 < stops:
            panel = passed_along(panel, "blk", 1)
    rows_energy = lax.dynamic_slice_in_dim(eps_virt, position * panel_rows, panel_rows, 0)
    denom = rows_energy[None, :, None] + eps_virt[None, None, :] - eps_pair[:, None, None]
    updated = (bare_ints.astype(jnp.float32) + cycle_sum) / denom * mask_cells.astype(jnp.float32)
    return updated.astype(jnp.bfloat16)


def solution(mesh):
    local = screened_exchange if mesh.shape["blk"] == 2 else ring_exchange
    in_specs = (
        P("own", "blk", None),
        P("own", "blk", None),
        P("own", "blk", None),
        P("blk", "own", None, None, None),
        P("blk", "own", None),
        P(),
        P("own"),
    )
    out_specs = P("own", "blk", None)
    return jax.shard_map(local, mesh=mesh, in_specs=in_specs, out_specs=out_specs, check_vma=False)
```

```python
import functools

import jax
import jax.numpy as jnp
from jax import lax
from jax.experimental import pallas as pl
from jax.experimental.pallas import tpu as pltpu
from jax.sharding import PartitionSpec as P

TILE = 128
NT = 24
STEP = 2
EARLY = 28
CHUNKS = (48, 40, 16)
SIZES = (16, 32, 40, 48, 64, 88, 120)
PAIR = 2
DEPTHS = (4, 6)
GROUP = 8
VMEM = 55 * 1024 * 1024


def passed_along(value, axis, steps):
    count = lax.axis_size(axis)
    pairs = [(source, (source + steps) % count) for source in range(count)]
    return lax.ppermute(value, axis, pairs)


def by24(index):
    return (index * 2731) >> 16


def make_plan(row_tiles, cap, early, where, info, plan_out):
    width = info.shape[1] // 2
    live = row_tiles * NT
    own, blk = where[0], where[1]
    infos = [info[:, :width], info[:, width:]]
    row = lax.broadcasted_iota(jnp.int32, (width, width), 0)
    lane = lax.broadcasted_iota(jnp.int32, (width, width), 1)
    row_hi, lane_hi = by24(row), by24(lane)
    row_lo, lane_lo = row - row_hi * NT, lane - lane_hi * NT
    same_lo = (row_lo == lane_lo).astype(jnp.float32)
    row_key, lane_key = row_lo * row_tiles + row_hi, lane_lo * row_tiles + lane_hi
    ahead = ((row_key < lane_key) & (row < live)).astype(jnp.bfloat16)
    places = lax.broadcasted_iota(jnp.int32, (8, width), 1)
    places_hi = by24(places)
    which = lax.broadcasted_iota(jnp.int32, (8, width), 0)
    digits = jnp.where(which == 0, places_hi, jnp.where(which == 1, places - places_hi * NT, 0))
    digits = digits.astype(jnp.bfloat16)
    owners = info.shape[0]
    mine = (lax.broadcasted_iota(jnp.int32, (owners, 1), 0) == own).astype(jnp.float32)
    lanes = lax.broadcasted_iota(jnp.int32, (owners, width), 1)

    def before(flags):
        return jnp.dot(flags.astype(jnp.bfloat16), ahead, preferred_element_type=jnp.float32)

    def listed(flags, count_before):
        count_column = jnp.sum(jnp.where(row == lane, count_before, 0.0), axis=1, keepdims=True)
        flag_column = jnp.sum(jnp.where(row == lane, flags, 0.0), axis=1, keepdims=True)
        onehot = jnp.where(count_column == lane.astype(jnp.float32), flag_column, 0.0)
        return jnp.dot(digits, onehot.astype(jnp.bfloat16), preferred_element_type=jnp.float32)

    masks = [
        jnp.broadcast_to(
            jnp.sum(jnp.where(lanes < live, info, 0).astype(jnp.float32) * mine, axis=0, keepdims=True), (8, width)
        )
        for info in infos
    ]

    most = jnp.int32(0)
    found = []
    for g in range(2):
        h = 1 - g
        seen = jnp.zeros((owners, width), jnp.float32)
        for slot in range(cap):
            seen = seen + (infos[g][:, live + slot : live + slot + 1] == lanes).astype(jnp.float32)
        seen = jnp.sum(seen, axis=0, keepdims=True)
        left = jnp.where(row_hi == lane_hi, seen, 0.0).astype(jnp.bfloat16)
        sender = 1 - blk if g == 0 else blk
        right = (row_lo == sender * row_tiles + lane_hi).astype(jnp.bfloat16)
        meets = jnp.dot(left, right, preferred_element_type=jnp.float32) * same_lo
        hits = jnp.dot(masks[g].astype(jnp.bfloat16), meets.astype(jnp.bfloat16), preferred_element_type=jnp.float32)
        need = jnp.where(hits > 0.5, masks[h], 0.0)
        kept_before = before(masks[h])
        late = jnp.where(kept_before >= early, need, 0.0)
        count = jnp.sum(late, axis=1, keepdims=True)
        most = jnp.maximum(most, jnp.max(count).astype(jnp.int32))
        found.append((late, before(late), count, kept_before))

    def write(lines):
        for index, line in lines.items():
            plan_out[index : index + 1, :] = jnp.broadcast_to(line[:1].astype(jnp.int32), (1, width))

    late, late_before, count, _ = found[1]
    sent_list = listed(late[:1], late_before[:1])
    write({0: sent_list[0:1], 1: sent_list[1:2], 2: count, 7: masks[0]})
    plan_out[11:12, :] = jnp.broadcast_to(most, (1, width))
    late, late_before, count, kept_before = found[0]
    late_list = listed(late[:1], late_before[:1])
    early_list = listed(masks[1][:1], kept_before[:1])
    total = jnp.sum(masks[1], axis=1, keepdims=True)
    write({3: late_list[0:1], 4: late_list[1:2], 5: late_before, 6: count})
    write({8: early_list[0:1], 9: early_list[1:2], 10: kept_before, 12: total})


def pack(plan, amps, targets, stage, sem):
    total = plan[2, 0]

    def tile_in(slot, place):
        row = pl.ds(pl.multiple_of(plan[0, slot] * TILE, TILE), TILE)
        column = pl.ds(pl.multiple_of(plan[1, slot] * TILE, TILE), TILE)
        return pltpu.make_async_copy(amps.at[0, row, column], stage.at[place], sem.at[0])

    def group_out(buf, group, place):
        return pltpu.make_async_copy(
            stage.at[pl.ds(place + group * GROUP, GROUP)], buf.at[pl.ds(group * GROUP, GROUP)], sem.at[1]
        )

    places = []
    place = 0
    for buf, start, stop in targets:
        end = jnp.clip(total, start, stop)

        def one(slot, carry, place=place, start=start):
            tile_in(slot, place + slot - start).start()
            return carry

        lax.fori_loop(start, end, one, 0)
        places.append((buf, place, end - start))
        place = place + buf.shape[0]
    for _, _, count in places:

        def landed(slot, carry):
            tile_in(0, 0).wait()
            return carry

        lax.fori_loop(0, count, landed, 0)
    groups = [(buf, place, (count + GROUP - 1) // GROUP) for buf, place, count in places]
    for buf, place, count in groups:

        def store(group, carry, buf=buf, place=place):
            group_out(buf, group, place).start()
            return carry

        lax.fori_loop(0, count, store, 0)
    for buf, place, count in groups:

        def stored(group, carry, buf=buf):
            group_out(buf, 0, 0).wait()
            return carry

        lax.fori_loop(0, count, stored, 0)


def pack_early(row_tiles, mask, amps, buf, stage, sem):
    count = buf.shape[0]

    def tile_in(place, column, at):
        rows = pl.ds(pl.multiple_of(place * TILE, TILE), TILE)
        lanes = pl.ds(pl.multiple_of(column * TILE, TILE), TILE)
        return pltpu.make_async_copy(amps.at[0, rows, lanes], stage.at[at], sem.at[0])

    def one_column(state):
        column, found = state
        for place in range(row_tiles):
            kept = (mask[0, place, column] > 0) & (found < count)
            pl.when(kept)(lambda place=place, found=found: tile_in(place, column, found).start())
            found = found + kept.astype(jnp.int32)
        return column + 1, found

    _, found = lax.while_loop(
        lambda state: (state[0] < NT) & (state[1] < count), one_column, (jnp.int32(0), jnp.int32(0))
    )

    def landed(index, carry):
        tile_in(0, 0, 0).wait()
        return carry

    lax.fori_loop(0, found, landed, 0)
    leaving = pltpu.make_async_copy(stage, buf, sem.at[1])
    leaving.start()
    leaving.wait()


def pack_extra(plan, amps, extra, stage, sem):
    pack(plan, amps, [(extra, jnp.int32(0), jnp.int32(extra.shape[0]))], stage, sem)


def pack_rest(cap, live, row_tiles, chunks, start, where, plan, labels, amps, *rest):
    bufs = rest[: len(chunks)]
    table, listed, stage, sem, found, counts = rest[len(chunks) :]
    targets = []
    for buf, size in zip(bufs, chunks):
        targets.append((buf, jnp.int32(start), jnp.int32(start + size)))
        start = start + size
    pack(plan, amps, targets, stage, sem)
    list_tiles(cap, live, row_tiles, where[1], labels, table, listed, found, counts)


def extra_sizes(most):
    return [size for size in SIZES if size < most] + [most]


def rest_of(most, chunks, sizes):
    over = most - sum(chunks)
    size = jnp.int32(sizes[0])
    for low, high in zip(sizes, sizes[1:]):
        size = jnp.where(over > low, high, size)
    return size


def place_kernel(part, whole, held, sem):
    coming = pltpu.make_async_copy(part, held, sem.at[0])
    coming.start()
    coming.wait()
    leaving = pltpu.make_async_copy(held, whole.at[pl.ds(0, held.shape[0])], sem.at[1])
    leaving.start()
    leaving.wait()


def placed(part, size):
    any_space = pl.BlockSpec(memory_space=pl.ANY)
    return pl.pallas_call(
        place_kernel,
        out_shape=jax.ShapeDtypeStruct((size,) + part.shape[1:], part.dtype),
        in_specs=[any_space],
        out_specs=any_space,
        scratch_shapes=[pltpu.VMEM(part.shape, part.dtype), pltpu.SemaphoreType.DMA((2,))],
        compiler_params=pltpu.CompilerParams(vmem_limit_bytes=16 * 1024 * 1024),
        name="placed",
    )(part)


def depth_for(pairs):
    depths = [depth for depth in DEPTHS if depth < NT // 2] + [NT // 2]
    wanted = jnp.int32(depths[0])
    for low, high in zip(depths, depths[1:]):
        wanted = jnp.where(pairs > low, high, wanted)
    return wanted, depths


def list_tiles(cap, live, row_tiles, blk, labels, table, listed, found, counts):
    blocks = row_tiles // PAIR

    def clear(block, carry):
        counts[block] = 0
        for column in range(NT):
            found[block, column] = -1
            table[block, column] = 0
        return carry

    lax.fori_loop(0, blocks, clear, 0)

    def of_owner(owner, count):
        for position in range(cap):
            label = labels[owner, live + position]

            @pl.when(label >= 0)
            def _(count=count):
                place = by24(label)
                column = label - place * NT - blk * row_tiles
                column = jnp.where(column < 0, column + NT, column)
                block = lax.shift_right_logical(place, 1)
                held = found[block, column]
                known = counts[block]
                at = jnp.where(held < 0, known, held)
                found[block, column] = at
                counts[block] = jnp.where(held < 0, known + 1, known)
                table[block, at] = column
                listed[0, count] = owner * cap + position
                listed[1, count] = place
                listed[2, count] = at

            count = count + (label >= 0).astype(jnp.int32)
        return count

    total = lax.fori_loop(0, labels.shape[0], of_owner, jnp.int32(0))
    pairs = lax.fori_loop(
        0, blocks, lambda block, most: jnp.maximum(most, (counts[block] + 1) // 2), jnp.int32(1)
    )
    table[blocks, 0] = pairs
    listed[3, 0] = total


def build_w(table, listed, tiles, w_out, w, sem):
    wanted, _ = depth_for(table[table.shape[0] - 1, 0])
    total = listed[3, 0]

    def zero(pair, carry):
        at = pl.ds(pl.multiple_of(pair * 2 * TILE, 2 * TILE), 2 * TILE)
        w[:, at] = jnp.zeros((w.shape[0], 2 * TILE), w.dtype)
        return carry

    lax.fori_loop(0, wanted, zero, 0)

    def tile_in(index):
        rows = pl.ds(pl.multiple_of(listed[1, index] * TILE, TILE), TILE)
        at = pl.ds(pl.multiple_of(listed[2, index] * TILE, TILE), TILE)
        return pltpu.make_async_copy(tiles.at[listed[0, index]], w.at[rows, at], sem.at[0])

    def start_in(index, carry):
        tile_in(index).start()
        return carry

    def landed(index, carry):
        tile_in(0).wait()
        return carry

    lax.fori_loop(0, total, start_in, 0)
    lax.fori_loop(0, total, landed, 0)

    def pair_out(pair):
        at = pl.ds(pl.multiple_of(pair * 2 * TILE, 2 * TILE), 2 * TILE)
        return pltpu.make_async_copy(w.at[:, at], w_out.at[:, at], sem.at[1])

    def start_out(pair, carry):
        pair_out(pair).start()
        return carry

    def left(pair, carry):
        pair_out(pair).wait()
        return carry

    lax.fori_loop(0, wanted, start_out, 0)
    lax.fori_loop(0, wanted, left, 0)


def cycle_kernel(
    row_tiles, early, chunks, sizes, stage, plan, table, energy, eps_row, eps_col, w_in,
    amps, bare, early_buf, prev_buf, this_buf, out_in, out, w, x, held, made, sems, w_sem,
):
    del out_in
    half = row_tiles * TILE
    pairs = table[row_tiles // PAIR, 0]
    steps = NT // STEP
    cols = STEP * TILE
    shift = rest_of(plan[11, 0], chunks, sizes)
    total = plan[6, 0]

    def slot_at(column):
        return jnp.where(column >= NT, total, plan[5, jnp.minimum(column, NT - 1)])

    def complete(limit):
        def one(step, count):
            return count + (slot_at((step + 1) * STEP) <= limit).astype(jnp.int32)

        return lax.fori_loop(0, steps, one, jnp.int32(0))

    ends = [jnp.int32(0)] + [shift + sum(chunks[:index]) for index in range(len(chunks) + 1)]
    begin = jnp.int32(0) if stage == 0 else complete(ends[stage])
    end = jnp.int32(steps) if stage == len(chunks) else complete(ends[stage + 1])
    split = ends[stage]
    prev_start = 0 if stage == 0 else ends[stage - 1]

    def dense_copies(step, slot):
        at = pl.ds(pl.multiple_of(step * cols, cols), cols)
        return (
            pltpu.make_async_copy(amps.at[0, :, at], x.at[slot, :half], sems.at[0, slot]),
            pltpu.make_async_copy(bare.at[0, :, at], held.at[slot], sems.at[1, slot]),
        )

    def out_copy(step, slot):
        at = pl.ds(pl.multiple_of(step * cols, cols), cols)
        return pltpu.make_async_copy(made.at[slot], out.at[0, :, at], sems.at[3, slot])

    def tile_copy(source, place, at, slot):
        rows = pl.ds(pl.multiple_of(half + place * TILE, TILE), TILE)
        return pltpu.make_async_copy(source, x.at[slot, rows, at * TILE : (at + 1) * TILE], sems.at[2, slot])

    def early_at(column):
        known = jnp.where(column >= NT, plan[12, 0], plan[10, jnp.minimum(column, NT - 1)])
        return jnp.minimum(known, early)

    def issue(step, slot):
        for copy in dense_copies(step, slot):
            copy.start()
        for at in range(STEP):
            column = step * STEP + at
            lanes = slice(at * TILE, (at + 1) * TILE)
            x[slot, half:, lanes] = jnp.zeros((half, TILE), x.dtype)
            low, high = slot_at(column), slot_at(column + 1)
            middle = jnp.clip(split, low, high)

            def from_buf(buf, base, line, at=at):
                def one(index, carry):
                    tile_copy(buf.at[index - base], plan[line, index], at, slot).start()
                    return carry

                return one

            lax.fori_loop(early_at(column), early_at(column + 1), from_buf(early_buf, 0, 8), 0)
            lax.fori_loop(low, middle, from_buf(prev_buf, prev_start, 3), 0)
            lax.fori_loop(middle, high, from_buf(this_buf, split, 3), 0)

    def masked(base, line, column, at, slot):
        for place in range(row_tiles):

            @pl.when(plan[line, place * NT + column] == 0)
            def _():
                rows = slice(base + place * TILE, base + (place + 1) * TILE)
                x[slot, rows, at * TILE : (at + 1) * TILE] = jnp.zeros((TILE, TILE), x.dtype)

    def arrive(step, slot):
        for copy in dense_copies(step, slot):
            copy.wait()
        for at in range(STEP):
            masked(0, 7, step * STEP + at, at, slot)

        def landed(index, carry):
            tile_copy(this_buf.at[0], 0, 0, slot).wait()
            return carry

        first, last = step * STEP, (step + 1) * STEP
        lax.fori_loop(0, early_at(last) - early_at(first) + slot_at(last) - slot_at(first), landed, 0)

    def product(step, slot, depth):
        at = pl.ds(pl.multiple_of(step * cols, cols), cols)
        for block in range(row_tiles // PAIR):
            rows = slice(block * PAIR * TILE, (block + 1) * PAIR * TILE)
            acc = None
            for pair in range(depth):
                pieces = []
                for index in (2 * pair, 2 * pair + 1):
                    place = pl.multiple_of(table[block, index] * TILE, TILE)
                    pieces.append(x[slot, pl.ds(place, TILE), :])
                part = jnp.dot(
                    w[rows, pair * 2 * TILE : (pair + 1) * 2 * TILE],
                    jnp.concatenate(pieces, axis=0),
                    preferred_element_type=jnp.float32,
                )
                acc = part if acc is None else acc + part
            denom = eps_row[rows, :] + eps_col[:, at] - energy[0]
            value = (held[slot, rows, :].astype(jnp.float32) + acc) / denom
            for part in range(PAIR):
                place = block * PAIR + part
                for column in range(STEP):
                    kept = plan[7, place * NT + step * STEP + column].astype(jnp.float32)
                    lanes = slice(column * TILE, (column + 1) * TILE)
                    piece = value[part * TILE : (part + 1) * TILE, lanes] * kept
                    made[slot, place * TILE : (place + 1) * TILE, lanes] = piece.astype(made.dtype)

    def w_copy(pair):
        at = pl.ds(pl.multiple_of(pair * 2 * TILE, 2 * TILE), 2 * TILE)
        return pltpu.make_async_copy(w_in.at[:, at], w.at[:, at], w_sem)

    @pl.when(begin < end)
    def _():
        wanted, depths = depth_for(pairs)

        def load(pair, carry):
            w_copy(pair).start()
            return carry

        lax.fori_loop(0, wanted, load, 0)
        issue(begin, lax.rem(begin, 2))

        def loaded(pair, carry):
            w_copy(pair).wait()
            return carry

        lax.fori_loop(0, wanted, loaded, 0)

        def one(step, carry):
            slot = lax.rem(step, 2)

            @pl.when(step + 1 < end)
            def _():
                issue(step + 1, 1 - slot)

            arrive(step, slot)

            @pl.when(step >= begin + 2)
            def _():
                out_copy(step - 2, slot).wait()

            for depth in depths:
                pl.when(wanted == depth)(functools.partial(product, step, slot, depth))
            out_copy(step, slot).start()
            return carry

        lax.fori_loop(begin, end, one, 0)

        @pl.when(end >= begin + 2)
        def _():
            out_copy(end - 2, lax.rem(end, 2)).wait()

        out_copy(end - 1, lax.rem(end - 1, 2)).wait()


def screened_exchange(amplitudes, amp_mask, bare_ints, int_tiles, tile_ids, eps_virt, eps_pair):
    pairs, panel_rows, width = amplitudes.shape
    row_tiles = panel_rows // TILE
    cap = tile_ids.shape[2]
    owners = lax.axis_size("own")
    own, blk = lax.axis_index("own"), lax.axis_index("blk")
    where = jnp.stack([own, blk]).astype(jnp.int32)
    early, chunks = EARLY, CHUNKS
    most_extra = row_tiles * NT - sum(chunks)
    sizes = extra_sizes(most_extra)
    any_space = pl.BlockSpec(memory_space=pl.ANY)
    in_hbm = pl.BlockSpec(memory_space=pltpu.HBM)
    smem = pl.BlockSpec(memory_space=pltpu.SMEM)
    vmem = pl.BlockSpec(memory_space=pltpu.VMEM)

    tiles = lax.all_gather(int_tiles, "own", axis=1, tiled=True).reshape(-1, TILE, TILE)

    live = row_tiles * NT
    wide = -(-(live + cap) // TILE) * TILE
    told = jnp.concatenate([amp_mask.reshape(1, -1), tile_ids.reshape(1, -1)], axis=1)
    told = jnp.pad(told, ((0, 0), (0, wide - live - cap)), constant_values=-1)
    partner_told = passed_along(told, "blk", 1)
    tile_type = lambda count: jax.ShapeDtypeStruct((count, TILE, TILE), amplitudes.dtype)
    params = pltpu.CompilerParams(vmem_limit_bytes=VMEM)
    light = pl.CostEstimate(flops=1, bytes_accessed=1, transcendentals=0)
    early_tiles = pl.pallas_call(
        functools.partial(pack_early, row_tiles),
        out_shape=tile_type(early),
        in_specs=[smem, in_hbm],
        out_specs=in_hbm,
        scratch_shapes=[pltpu.VMEM((early, TILE, TILE), amplitudes.dtype), pltpu.SemaphoreType.DMA((2,))],
        compiler_params=params,
        cost_estimate=light,
        name="pack_early",
    )(amp_mask, amplitudes)
    partner_told, early_tiles = lax.optimization_barrier((partner_told, early_tiles))
    early_buf = passed_along(early_tiles, "blk", 1)
    told = jnp.broadcast_to(jnp.concatenate([told, partner_told], axis=1), (owners, 2 * wide))
    info = lax.all_to_all(told, "own", 0, 0, tiled=True)

    plan = pl.pallas_call(
        functools.partial(make_plan, row_tiles, cap, early),
        out_shape=jax.ShapeDtypeStruct((16, wide), jnp.int32),
        in_specs=[smem, vmem],
        out_specs=vmem,
        compiler_params=params,
        cost_estimate=light,
        name="make_plan",
    )(where, info)
    blocks = row_tiles // PAIR
    labels = info[:, :wide]

    def branch(size):
        def send(where, plan, labels, amplitudes):
            extra = pl.pallas_call(
                pack_extra,
                out_shape=tile_type(size),
                in_specs=[smem, in_hbm],
                out_specs=in_hbm,
                scratch_shapes=[
                    pltpu.VMEM((size, TILE, TILE), amplitudes.dtype),
                    pltpu.SemaphoreType.DMA((2,)),
                ],
                compiler_params=params,
                cost_estimate=light,
                name="pack_extra",
            )(plan, amplitudes)
            moved = passed_along(extra, "blk", 1)
            *others, table, listed = pl.pallas_call(
                functools.partial(pack_rest, cap, live, row_tiles, chunks, size),
                out_shape=[tile_type(count) for count in chunks]
                + [
                    jax.ShapeDtypeStruct((blocks + 1, NT), jnp.int32),
                    jax.ShapeDtypeStruct((4, owners * cap), jnp.int32),
                ],
                in_specs=[smem, smem, smem, in_hbm],
                out_specs=[in_hbm] * len(chunks) + [smem, smem],
                scratch_shapes=[
                    pltpu.VMEM((sum(chunks), TILE, TILE), amplitudes.dtype),
                    pltpu.SemaphoreType.DMA((2,)),
                    pltpu.SMEM((blocks, NT), jnp.int32),
                    pltpu.SMEM((blocks,), jnp.int32),
                ],
                compiler_params=params,
                cost_estimate=light,
                name="pack_rest",
            )(where, plan, labels, amplitudes)
            return (placed(moved, sizes[-1]), table, listed, *others)

        return send

    place = sum((plan[11, 0] - sum(chunks) > size).astype(jnp.int32) for size in sizes[:-1])
    got, table, listed, *others = lax.switch(
        place, [branch(size) for size in sizes], where, plan, labels, amplitudes
    )
    got, first = lax.optimization_barrier((got, others[0]))
    bufs = [got, passed_along(first, "blk", 1)]
    w = pl.pallas_call(
        build_w,
        out_shape=jax.ShapeDtypeStruct((panel_rows, width), jnp.bfloat16),
        in_specs=[smem, smem, any_space],
        out_specs=in_hbm,
        scratch_shapes=[pltpu.VMEM((panel_rows, width), jnp.bfloat16), pltpu.SemaphoreType.DMA((2,))],
        compiler_params=params,
        name="build_w",
    )(table, listed, tiles)
    w, second = lax.optimization_barrier((w, others[1]))
    bufs.append(passed_along(second, "blk", 1))
    eps_row = lax.dynamic_slice_in_dim(eps_virt, blk * panel_rows, panel_rows, 0).reshape(panel_rows, 1)
    eps_col = eps_virt.reshape(1, width)
    cols = STEP * TILE
    out = None
    for stage in range(len(chunks) + 1):
        prev_buf = bufs[max(stage - 1, 0)]
        operands = [
            plan, table, eps_pair, eps_row, eps_col, w, amplitudes, bare_ints, early_buf,
            prev_buf, bufs[stage], bare_ints if out is None else out,
        ]
        out = pl.pallas_call(
            functools.partial(cycle_kernel, row_tiles, early, chunks, sizes, stage),
            out_shape=jax.ShapeDtypeStruct(amplitudes.shape, amplitudes.dtype),
            in_specs=[smem] * 3 + [vmem] * 2 + [any_space] + [in_hbm] * 2 + [any_space] * 3 + [in_hbm],
            out_specs=in_hbm,
            input_output_aliases={} if out is None else {11: 0},
            scratch_shapes=[
                pltpu.VMEM((panel_rows, width), jnp.bfloat16),
                pltpu.VMEM((2, width, cols), jnp.bfloat16),
                pltpu.VMEM((2, panel_rows, cols), jnp.bfloat16),
                pltpu.VMEM((2, panel_rows, cols), jnp.bfloat16),
                pltpu.SemaphoreType.DMA((4, 2)),
                pltpu.SemaphoreType.DMA,
            ],
            compiler_params=params,
            cost_estimate=pl.CostEstimate(
                flops=2 * panel_rows * width * width // len(chunks),
                bytes_accessed=4 * panel_rows * width * 2 // len(chunks),
                transcendentals=0,
            ),
            name=f"cycle_{stage}",
        )(*operands)
        if len(bufs) < len(chunks) + 1:
            out, following = lax.optimization_barrier((out, others[len(bufs) - 1]))
            bufs.append(passed_along(following, "blk", 1))
    return out


def ring_exchange(amplitudes, amp_mask, bare_ints, int_tiles, tile_ids, eps_virt, eps_pair):
    pairs, panel_rows, width = amplitudes.shape
    row_tiles = panel_rows // TILE
    slots = row_tiles * NT
    mask_cells = jnp.broadcast_to(
        amp_mask.astype(jnp.bfloat16)[:, :, None, :, None], (pairs, row_tiles, TILE, NT, TILE)
    ).reshape(pairs, panel_rows, width)
    screened = amplitudes * mask_cells
    tiles = lax.all_gather(int_tiles, "own", axis=1, tiled=True)
    labels = lax.all_gather(tile_ids, "own", axis=1, tiled=True)
    flat_labels = labels.reshape(-1)
    flat_tiles = tiles.reshape(-1, TILE, TILE)
    onehot = (flat_labels[:, None] == jnp.arange(slots, dtype=jnp.int32)[None, :]).astype(jnp.bfloat16)
    grid = jnp.einsum("sq,sij->qij", onehot, flat_tiles, preferred_element_type=jnp.float32)
    w_rows = (
        grid.astype(jnp.bfloat16)
        .reshape(row_tiles, NT, TILE, TILE)
        .transpose(0, 2, 1, 3)
        .reshape(panel_rows, width)
    )
    position = lax.axis_index("blk")
    stops = lax.axis_size("blk")
    panel = screened
    cycle_sum = jnp.zeros((pairs, panel_rows, width), jnp.float32)
    for stop in range(stops):
        columns = lax.dynamic_slice_in_dim(w_rows, (position - stop) % stops * panel_rows, panel_rows, 1)
        cycle_sum = cycle_sum + jnp.einsum("ac,pcb->pab", columns, panel, preferred_element_type=jnp.float32)
        if stop + 1 < stops:
            panel = passed_along(panel, "blk", 1)
    rows_energy = lax.dynamic_slice_in_dim(eps_virt, position * panel_rows, panel_rows, 0)
    denom = rows_energy[None, :, None] + eps_virt[None, None, :] - eps_pair[:, None, None]
    updated = (bare_ints.astype(jnp.float32) + cycle_sum) / denom * mask_cells.astype(jnp.float32)
    return updated.astype(jnp.bfloat16)


def solution(mesh):
    local = screened_exchange if mesh.shape["blk"] == 2 else ring_exchange
    in_specs = (
        P("own", "blk", None),
        P("own", "blk", None),
        P("own", "blk", None),
        P("blk", "own", None, None, None),
        P("blk", "own", None),
        P(),
        P("own"),
    )
    out_specs = P("own", "blk", None)
    return jax.shard_map(local, mesh=mesh, in_specs=in_specs, out_specs=out_specs, check_vma=False)
```
